512 devices in a mesh: dp: 64 (over y, x, core), expert: 8 (over z).
Axes of the slice: x: 4, y: 8, z: 8, core: 2. Of those that a mesh axis runs over, the one named last changes fastest.
Arguments:
- att_input: bfloat16 [24576, 4096], P('dp', 'expert'), may hold values from -6 to 6
- kv_cotangent: bfloat16 [24576, 1024], P('dp')
- expert_hidden: bfloat16 [3072, 12288], P('expert', 'dp')
- expert_cotangent: bfloat16 [3072, 131072], P('expert', 'dp'), may hold values from -6 to 6
- token_counts: int32 [64, 8], P('dp', 'expert'), may hold values from 1 to 384, 1728 in all within a row
- att_param: float32 [1024, 4096], P('dp', 'expert'), may hold values from -4 to 4
- att_moment: float32 [1024, 4096], P('dp', 'expert'), may hold values from -6 to 6
- att_second: float32 [1024, 4096], P('dp', 'expert'), may hold values from 0.2 to 4
- exp_param: float32 [12288, 2048], P(('dp', 'expert')), may hold values from -4 to 4
- exp_moment: float32 [12288, 2048], P(('dp', 'expert')), may hold values from -6 to 6
- exp_second: float32 [12288, 2048], P(('dp', 'expert')), may hold values from 0.2 to 4
Outputs:
- new_att_param: float32 [1024, 4096], P('dp', 'expert')
- new_att_moment: float32 [1024, 4096], P('dp', 'expert')
- new_att_second: float32 [1024, 4096], P('dp', 'expert')
- new_exp_param: float32 [12288, 2048], P(('dp', 'expert'))
- new_exp_moment: float32 [12288, 2048], P(('dp', 'expert'))
- new_exp_second: float32 [12288, 2048], P(('dp', 'expert'))
The draws below stay inside these ranges and needn't reach their ends.
Inputs may be any that keep to these rules, and one draw needn't show every extreme that they name: Each row of token_counts sums to 1728, and its largest entry is 384.
All inputs are finite; a program needn't handle non-finite values. No bound on the sum of `token_counts` on one device may be relied on, other than what follows from the above.
Results may differ from the reference program's by a relative error of at most 0.0003.
Values sent between devices are 32-bit elements; how exact they have to be, the bound alone decides.
A program may use at most 64 MiB of HBM per device.

```python
import math
import jax
import jax.numpy as jnp
import numpy as np
from jax import lax

D = 4096
KV2 = 1024
FF = 1536
DW = 2048
GROUP = 8
TOK_DEV = 384
EXPERTS = 8
ATT_TOK = 24576
EXP_TOK = 3072
N_DP = 64
N_EXPERT = 8


def spread_scales(base, key, rise):
    row_key, col_key = jax.random.split(key)
    height, width = base.shape
    row_scale = 10.0 ** (jax.random.uniform(row_key, (height, 1), jnp.float32) - 0.5)
    ramp = jnp.exp(rise * jnp.arange(width, dtype=jnp.float32) / (width - 1))
    col_scale = 10.0 ** (jax.random.uniform(col_key, (1, width), jnp.float32) - 0.5) * ramp[None, :] / math.sqrt(3.0)
    return base * row_scale * col_scale


def draw_kv_cotangent(key, part):
    key = jax.random.fold_in(key, 11)
    base_key, scale_key = jax.random.split(key)
    base = jax.random.normal(base_key, (ATT_TOK, KV2), jnp.float32)
    return spread_scales(base, scale_key, math.log(3.0)).astype(jnp.bfloat16)


def draw_expert_hidden(key, part):
    key = jax.random.fold_in(key, 23)
    base_key, scale_key = jax.random.split(key)
    base = jax.random.normal(base_key, (EXP_TOK, EXPERTS * FF), jnp.float32)
    return spread_scales(base, scale_key, math.log(3.0)).astype(jnp.bfloat16)


def steps_of(key, extent, cuts, low, top_value):
    level, own = 1.0, jax.random.fold_in(key, 6)
    for position, shards_of in cuts:
        heights = jnp.exp(jax.random.uniform(jax.random.fold_in(own, position), (shards_of,), jnp.float32, low / len(cuts), top_value / len(cuts)))
        level = level * jnp.repeat(heights, extent[position] // shards_of).reshape([-1 if axis == position else 1 for axis in range(len(extent))])
    return level


def profile(number_of, total, bound, slope):
    weights = [(1 << 20) // math.isqrt(rank ** slope) + 1 for rank in range(2, number_of + 1)]
    spare, holding = total - bound - (number_of - 1), [1] * (number_of - 1)
    while spare > 0:
        candidates = [i for i in range(number_of - 1) if holding[i] < bound]
        pool, left = sum([weights[i] for i in candidates]), spare
        for i in candidates:
            addition = min(bound - holding[i], max(1, left * weights[i] // pool), spare)
            holding[i] = holding[i] + addition
            spare = spare - addition
    return np.array([bound] + holding)


def uneven(rng, number_of, total, most, lean):
    if number_of == 2:
        one = jax.random.randint(rng, (), max(1, total - most), min(most, total - 1) + 1)
        return jnp.stack([one, total - one])
    tallies = jnp.asarray(profile(number_of, total, most, lean), jnp.int32)
    pairs = (number_of - 1) // 2
    donor, receiver = tallies[1:1 + 2 * pairs:2], tallies[2:2 + 2 * pairs:2]
    room = jnp.minimum(donor - 1, most - receiver)
    moved = jax.random.randint(jax.random.fold_in(rng, 1), (pairs,), 0, 1 << 20) % (room + 1)
    tallies = tallies.at[1:1 + 2 * pairs:2].set(donor - moved).at[2:2 + 2 * pairs:2].set(receiver + moved)
    return tallies[jax.random.permutation(jax.random.fold_in(rng, 2), number_of)]


def noise(key, dims, scale, limit, shards=(), held_as=jnp.bfloat16):
    values = jax.random.normal(key, dims, jnp.float32) * scale
    if len(shards) > 0:
        values = steps_of(key, dims, shards, -0.22, 0.18) * values
    return jnp.clip(values, min=-limit, max=limit).astype(held_as)


def setup_inputs(seed: int = 0) -> dict:
    key_of = jax.random.split(jax.random.key(seed), 12)
    return {
        "att_input": noise(key_of[0], (ATT_TOK, D), 1.0, 6.0, ((0, 64), (1, 8))),
        "kv_cotangent": draw_kv_cotangent(jax.random.fold_in(key_of[11], 71), 0),
        "expert_hidden": draw_expert_hidden(jax.random.fold_in(key_of[11], 71), 0),
        "expert_cotangent": noise(key_of[3], (EXP_TOK, N_DP * DW), 1.0, 6.0, ((0, 8), (1, 64))),
        "token_counts": jax.vmap(lambda own: uneven(own, N_EXPERT, TOK_DEV * (N_EXPERT + 1) // 2, TOK_DEV, 2))(jax.random.split(key_of[4], N_DP)).reshape((N_DP, N_EXPERT)).astype(jnp.int32),
        "att_param": noise(key_of[5], (KV2, D), 0.5, 4.0, ((0, 64), (1, 8)), jnp.float32),
        "att_moment": noise(key_of[6], (KV2, D), 1.0, 6.0, ((0, 64), (1, 8)), jnp.float32),
        "att_second": jnp.clip(jnp.exp(math.log(4.0) - 2.9957323 * jax.random.uniform(key_of[7], (KV2, D), jnp.float32) ** steps_of(key_of[7], (KV2, D), ((0, 64), (1, 8)), -0.2, 0.2)), 0.2, 4.0),
        "exp_param": noise(key_of[8], (EXPERTS * FF, DW), 0.5, 4.0, ((0, 512),), jnp.float32),
        "exp_moment": noise(key_of[9], (EXPERTS * FF, DW), 1.0, 6.0, ((0, 512),), jnp.float32),
        "exp_second": jnp.clip(jnp.exp(math.log(4.0) - 2.9957323 * jax.random.uniform(key_of[10], (EXPERTS * FF, DW), jnp.float32) ** steps_of(key_of[10], (EXPERTS * FF, DW), ((0, 512),), -0.2, 0.2)), 0.2, 4.0),
    }


beta_one = 0.9
beta_two = 0.95
learn_rate = 0.01
decay_rate = 0.1
epsilon = 1e-08
step_number = 5

def adam_update(param, moment, second, grad, clip):
    scaled = clip * grad
    new_moment = beta_one * moment + (1.0 - beta_one) * scaled
    new_second = beta_two * second + (1.0 - beta_two) * scaled * scaled
    fix_one = 1.0 - beta_one ** step_number
    fix_two = 1.0 - beta_two ** step_number
    update = new_moment / fix_one / (jnp.sqrt(new_second / fix_two) + epsilon)
    new_param = param - learn_rate * (update + decay_rate * param)
    return (new_param, new_moment, new_second)

def reference(att_input, kv_cotangent, expert_hidden, expert_cotangent, token_counts, att_param, att_moment, att_second, exp_param, exp_moment, exp_second):
    att_grad = lax.dot_general(kv_cotangent, att_input, (((0,), (0,)), ((), ())), preferred_element_type=jnp.float32)
    slab = FF // GROUP
    hidden_blocks = expert_hidden.reshape(N_EXPERT, TOK_DEV, N_DP, slab)
    cotangent_blocks = expert_cotangent.reshape(N_EXPERT, TOK_DEV, N_DP, DW)
    positions = jnp.arange(TOK_DEV, dtype=jnp.int32)
    live_rows = positions[None, :, None] < jnp.transpose(token_counts)[:, None, :]
    masked_hidden = jnp.where(live_rows[..., None], hidden_blocks, jnp.zeros((), jnp.bfloat16))

    def one_block(device):
        hidden_part = lax.dynamic_index_in_dim(masked_hidden, device, axis=2, keepdims=False).reshape(N_EXPERT * TOK_DEV, slab)
        cot_part = lax.dynamic_index_in_dim(cotangent_blocks, device, axis=2, keepdims=False).reshape(N_EXPERT * TOK_DEV, DW)
        return lax.dot_general(hidden_part, cot_part, (((0,), (0,)), ((), ())), preferred_element_type=jnp.float32)
    exp_grad = lax.map(one_block, jnp.arange(N_DP, dtype=jnp.int32)).reshape(N_DP * slab, DW)
    square_sum = jnp.sum(att_grad * att_grad) + jnp.sum(exp_grad * exp_grad)
    entries = float(KV2 * D + EXPERTS * FF * DW)
    clip = jnp.minimum(1.0, jnp.sqrt(entries) / (jnp.sqrt(square_sum) + 1e-06))
    new_att = adam_update(att_param, att_moment, att_second, att_grad, clip)
    new_exp = adam_update(exp_param, exp_moment, exp_second, exp_grad, clip)
    return (new_att[0], new_att[1], new_att[2], new_exp[0], new_exp[1], new_exp[2])
```

```python
import functools

import jax
import jax.numpy as jnp
from jax import lax
from jax.experimental import pallas as pl
from jax.experimental.pallas import tpu as pltpu
from jax.sharding import PartitionSpec as P

D = 4096
KV2 = 1024
FF = 1536
DW = 2048
GROUP = 8

beta_one = 0.9
beta_two = 0.95
learn_rate = 0.01
decay_rate = 0.1
epsilon = 1e-08
step_number = 5

NX, NY, NZ, NC = 4, 8, 8, 2
TOK = 384
HID = 192
OWN = HID // NZ
PIECES = 4
WIDE = DW // PIECES
COLS = 512
HALF = COLS // 2
ROWS = 16
GROUPS = 4
Y_ORDER = (4, 3, 5, 2, 6, 1, 7, 0)
NORM_STEPS = ((NZ, 1, 1, 1), (1, NY, 1, 1), (1, 1, NX, NC))
NORM_PEERS = tuple(a * b * c * d for a, b, c, d in NORM_STEPS)
MESH = pl.DeviceIdType.MESH


def grads_kernel(
    hidden_hbm, cot_hbm, kv_hbm, x_hbm, count_ref,
    exp_ref, att_ref, norm_ref,
    hidden, cot, kv, xin, masked, part, ring, grad, core_in, keep, send_a, recv_a, keep_b, send_b, recv_b, y_out, y_in,
    norm_a, norm_b, norm_c,
    load_sem, ring_send, ring_recv, core_send, core_recv, a_send, a_recv, b_send, b_recv, y_send, y_recv, norm_send, norm_recv,
):
    dp = lax.axis_index("dp")
    z = lax.axis_index("expert")
    c = lax.rem(dp, NC)
    x = lax.rem(dp // NC, NX)
    y = dp // (NC * NX)

    def at(zz, yy, xx, cc):
        return ((yy * NX + xx) * NC + cc, zz)

    x_rel = (x, x + 1 - 2 * lax.rem(x, 2), lax.rem(x + 2, NX), NX - 1 - x)

    barrier = pltpu.get_barrier_semaphore()
    greeted = [at(lax.rem(z + 1, NZ), y, x, c), at(lax.rem(z + NZ - 1, NZ), y, x, c), at(z, y, x, 1 - c)]
    greeted += [at(z, y, x_rel[1], c), at(z, y, x_rel[3], c)]
    greeted += [at(z, lax.rem(y + d, NY), x, c) for d in range(1, NY)]
    for device in greeted:
        pl.semaphore_signal(barrier, inc=1, device_id=device, device_id_type=MESH)

    loads = [pltpu.make_async_copy(hidden_hbm, hidden, load_sem.at[0])]
    for k in range(PIECES):
        loads.append(pltpu.make_async_copy(cot_hbm.at[:, pl.ds(k * WIDE, WIDE)], cot.at[k], load_sem.at[1 + k]))
    loads.append(pltpu.make_async_copy(x_hbm, xin, load_sem.at[1 + PIECES]))
    loads.append(pltpu.make_async_copy(kv_hbm, kv, load_sem.at[2 + PIECES]))
    for load in loads:
        load.start()

    sends = []

    def remote(src, dst, send_sem, recv_sem, device):
        copy = pltpu.make_async_remote_copy(
            src_ref=src, dst_ref=dst, send_sem=send_sem, recv_sem=recv_sem, device_id=device, device_id_type=MESH
        )
        copy.start()
        sends.append(copy)
        return copy

    def shard(k, t):
        return lax.rem(z + NZ - 1 - t, NZ) if k % 2 == 0 else lax.rem(z + 1 + t, NZ)

    def ring_to(k):
        return at(lax.rem(z + 1, NZ) if k % 2 == 0 else lax.rem(z + NZ - 1, NZ), y, x, c)

    arrivals = {}

    def ring_send_step(k, t):
        src = part.at[k, shard(k, 0)] if t == 0 else ring.at[k, t - 1]
        arrivals[k, t] = remote(src, ring.at[k, t], ring_send.at[k, t], ring_recv.at[k, t], ring_to(k))

    def ring_step(k, t):
        arrivals[k, t].wait_recv()
        ring[k, t] = ring[k, t] + part[k, shard(k, t + 1)]
        ring_send_step(k, t + 1)

    loads[0].wait()
    live = lax.broadcasted_iota(jnp.int32, (TOK, HID), 0) < count_ref[0, 0]
    masked[...] = jnp.where(live, hidden[...].astype(jnp.float32), 0.0).astype(jnp.bfloat16)

    def exp_piece(k):
        loads[1 + k].wait()
        block = lax.dot_general(
            masked[...], cot[k], (((0,), (0,)), ((), ())), preferred_element_type=jnp.float32
        )
        part[k] = block.reshape(NZ, OWN, WIDE)
        if k == 0:
            pl.semaphore_wait(barrier, len(greeted))
        ring_send_step(k, 0)

    core_copy, a_copy, b_copy = {}, {}, {}

    def att_group(g):
        if g == 0:
            loads[1 + PIECES].wait()
            loads[2 + PIECES].wait()
        for i in (2 * g, 2 * g + 1):
            target = lax.rem(y + Y_ORDER[i], NY)
            columns = kv[:, pl.ds(pl.multiple_of(target * (KV2 // NY), KV2 // NY), KV2 // NY)]
            block = lax.dot_general(columns, xin[...], (((0,), (0,)), ((), ())), preferred_element_type=jnp.float32)
            grad[i] = block.reshape(NX, NC, ROWS, COLS)
        core_copy[g] = remote(
            grad.at[pl.ds(2 * g, 2), :, 1 - c], core_in.at[g], core_send.at[g], core_recv.at[g], at(z, y, x, 1 - c)
        )

    slots = ((0, 3, 1, 2), (0, 1, 3, 2))
    first_to = (x_rel[1], x_rel[3])
    second_to = (x_rel[3], x_rel[1])

    def att_first(g):
        core_copy[g].wait_recv()
        for h in range(2):
            cols = pl.ds(h * HALF, HALF)
            for j in (2, 3):
                at_x = x_rel[slots[h][j]]
                for i in range(2):
                    send_a[g, h, j - 2, i] = grad[2 * g + i, at_x, c, :, cols] + core_in[g, i, at_x, :, cols]
            a_copy[g, h] = remote(
                send_a.at[g, h], recv_a.at[g, h], a_send.at[g, h], a_recv.at[g, h], at(z, y, first_to[h], c)
            )
        for h in range(2):
            cols = pl.ds(h * HALF, HALF)
            for j in (0, 1):
                at_x = x_rel[slots[h][j]]
                for i in range(2):
                    keep[g, h, j, i] = grad[2 * g + i, at_x, c, :, cols] + core_in[g, i, at_x, :, cols]

    def att_second(g):
        for h in range(2):
            a_copy[g, h].wait_recv()
            send_b[g, h] = keep[g, h, 1] + recv_a[g, h, 1]
            b_copy[g, h] = remote(
                send_b.at[g, h], recv_b.at[g, h], b_send.at[g, h], b_recv.at[g, h], at(z, y, second_to[h], c)
            )
            keep_b[g, h] = keep[g, h, 0] + recv_a[g, h, 0]

    y_copy = {}

    def att_third(g):
        for h in range(2):
            b_copy[g, h].wait_recv()
            for i in range(2):
                y_out[2 * g + i, :, pl.ds(h * HALF, HALF)] = keep_b[g, h, i] + recv_b[g, h, i]
        for i in (2 * g, 2 * g + 1):
            d = Y_ORDER[i]
            if d:
                y_copy[d] = remote(
                    y_out.at[i], y_in.at[d - 1], y_send.at[d - 1], y_recv.at[d - 1], at(z, lax.rem(y + d, NY), x, c)
                )

    def att_last():
        total = y_out[Y_ORDER.index(0)]
        for d in Y_ORDER:
            if d:
                y_copy[d].wait_recv()
                total = total + y_in[d - 1]
        att_ref[...] = total
        return jnp.sum(total * total, axis=0, keepdims=True)

    def steps(t, *pieces):
        for k in pieces or range(PIECES):
            ring_step(k, t)

    for k in range(PIECES):
        exp_piece(k)
    att_group(0)
    att_group(1)
    steps(0, 0, 1)
    att_group(2)
    steps(0, 2, 3)
    att_group(3)
    att_first(0)
    steps(1, 0, 1)
    att_first(1)
    steps(1, 2, 3)
    att_first(2)
    steps(2, 0, 1)
    att_first(3)
    att_second(0)
    steps(2, 2, 3)
    att_second(1)
    steps(3, 0, 1)
    att_second(2)
    att_third(0)
    steps(3, 2, 3)
    att_third(1)
    steps(4, 0, 1)
    att_second(3)
    att_third(2)
    steps(4, 2, 3)
    steps(5, 0, 1)
    att_third(3)
    steps(5, 2, 3)

    att_squares = att_last()
    squares = att_squares[:, 0:128]
    for j in range(1, COLS // 128):
        squares = squares + att_squares[:, j * 128 : (j + 1) * 128]
    for k in range(PIECES):
        arrivals[k, NZ - 2].wait_recv()
        total = ring[k, NZ - 2] + part[k, z]
        exp_ref[:, pl.ds(k * WIDE, WIDE)] = total
        sums = jnp.sum(total * total, axis=0, keepdims=True)
        for j in range(WIDE // 128):
            squares = squares + sums[:, j * 128 : (j + 1) * 128]

    value = squares
    for n, (extent, peers, buffer) in enumerate(zip(NORM_STEPS, NORM_PEERS, (norm_a, norm_b, norm_c))):
        buffer[0] = value
        slot = 0
        for dz in range(extent[0]):
            for dy in range(extent[1]):
                for dx in range(extent[2]):
                    for dc in range(extent[3]):
                        if slot:
                            device = at(
                                lax.rem(z + dz, NZ), lax.rem(y + dy, NY), lax.rem(x + dx, NX), lax.rem(c + dc, NC)
                            )
                            pltpu.make_async_remote_copy(
                                src_ref=buffer.at[0],
                                dst_ref=buffer.at[slot],
                                send_sem=norm_send.at[n],
                                recv_sem=norm_recv.at[n],
                                device_id=device,
                                device_id_type=MESH,
                            ).start()
                        slot += 1
        others = buffer.at[pl.ds(1, peers - 1)]
        pltpu.make_async_copy(others, others, norm_recv.at[n]).wait()
        value = jnp.sum(buffer[...], axis=0)
    norm_ref[...] = value

    for copy in sends:
        copy.wait_send()
    for n, (peers, buffer) in enumerate(zip(NORM_PEERS, (norm_a, norm_b, norm_c))):
        others = buffer.at[pl.ds(1, peers - 1)]
        pltpu.make_async_copy(others, others, norm_send.at[n]).wait()


def grads(hidden, cot, kv, xin, counts):
    f32, bf16 = jnp.float32, jnp.bfloat16
    dma = pltpu.SemaphoreType.DMA
    hbm = pl.BlockSpec(memory_space=pl.ANY)
    vmem = pl.BlockSpec(memory_space=pltpu.VMEM)
    return pl.pallas_call(
        grads_kernel,
        out_shape=(
            jax.ShapeDtypeStruct((OWN, DW), f32),
            jax.ShapeDtypeStruct((ROWS, COLS), f32),
            jax.ShapeDtypeStruct((1, 128), f32),
        ),
        in_specs=[hbm, hbm, hbm, hbm, pl.BlockSpec(memory_space=pltpu.SMEM)],
        out_specs=(vmem, vmem, vmem),
        scratch_shapes=[
            pltpu.VMEM((TOK, HID), bf16),
            pltpu.VMEM((PIECES, TOK, WIDE), bf16),
            pltpu.VMEM((TOK, KV2), bf16),
            pltpu.VMEM((TOK, COLS), bf16),
            pltpu.VMEM((TOK, HID), bf16),
            pltpu.VMEM((PIECES, NZ, OWN, WIDE), f32),
            pltpu.VMEM((PIECES, NZ - 1, OWN, WIDE), f32),
            pltpu.VMEM((NY, NX, NC, ROWS, COLS), f32),
            pltpu.VMEM((GROUPS, 2, NX, ROWS, COLS), f32),
            pltpu.VMEM((GROUPS, 2, 2, 2, ROWS, HALF), f32),
            pltpu.VMEM((GROUPS, 2, 2, 2, ROWS, HALF), f32),
            pltpu.VMEM((GROUPS, 2, 2, 2, ROWS, HALF), f32),
            pltpu.VMEM((GROUPS, 2, 2, ROWS, HALF), f32),
            pltpu.VMEM((GROUPS, 2, 2, ROWS, HALF), f32),
            pltpu.VMEM((GROUPS, 2, 2, ROWS, HALF), f32),
            pltpu.VMEM((NY, ROWS, COLS), f32),
            pltpu.VMEM((NY - 1, ROWS, COLS), f32),
            pltpu.VMEM((NORM_PEERS[0], 1, 128), f32),
            pltpu.VMEM((NORM_PEERS[1], 1, 128), f32),
            pltpu.VMEM((NORM_PEERS[2], 1, 128), f32),
            dma((3 + PIECES,)),
            dma((PIECES, NZ - 1)),
            dma((PIECES, NZ - 1)),
            dma((GROUPS,)),
            dma((GROUPS,)),
            dma((GROUPS, 2)),
            dma((GROUPS, 2)),
            dma((GROUPS, 2)),
            dma((GROUPS, 2)),
            dma((NY - 1,)),
            dma((NY - 1,)),
            dma((3,)),
            dma((3,)),
        ],
        compiler_params=pltpu.CompilerParams(
            collective_id=0, has_side_effects=True, vmem_limit_bytes=24 * 1024 * 1024
        ),
        name="grads",
    )(hidden, cot, kv, xin, counts)


def adam_update(param, moment, second, grad, clip):
    scaled = clip * grad
    new_moment = beta_one * moment + (1.0 - beta_one) * scaled
    new_second = beta_two * second + (1.0 - beta_two) * scaled * scaled
    fix_one = 1.0 - beta_one**step_number
    fix_two = 1.0 - beta_two**step_number
    update = new_moment / fix_one / (jnp.sqrt(new_second / fix_two) + epsilon)
    new_param = param - learn_rate * (update + decay_rate * param)
    return (new_param, new_moment, new_second)


def update_kernel(norm_ref, *refs):
    entries = float(KV2 * D + NY * NX * NC // GROUP * FF * DW)
    square_sum = jnp.sum(norm_ref[...], axis=1, keepdims=True)
    clip = jnp.minimum(1.0, jnp.sqrt(jnp.full_like(square_sum, entries)) / (jnp.sqrt(square_sum) + 1e-06))
    for n in range(2):
        param, moment, second, grad = refs[4 * n : 4 * n + 4]
        new = adam_update(param[...], moment[...], second[...], grad[...], clip)
        for ref, value in zip(refs[8 + 3 * n : 11 + 3 * n], new):
            ref[...] = value


def update(norm, att, exp):
    shapes = [jax.ShapeDtypeStruct(a.shape, a.dtype) for a in (*att[:3], *exp[:3])]
    vmem = pl.BlockSpec(memory_space=pltpu.VMEM)
    return pl.pallas_call(
        update_kernel,
        out_shape=tuple(shapes),
        in_specs=[vmem] * 9,
        out_specs=(vmem,) * 6,
        name="update",
    )(norm, *att, *exp)


def on_device(
    att_input,
    kv_cotangent,
    expert_hidden,
    expert_cotangent,
    token_counts,
    att_param,
    att_moment,
    att_second,
    exp_param,
    exp_moment,
    exp_second,
):
    exp_grad, att_grad, norm = grads(expert_hidden, expert_cotangent, kv_cotangent, att_input, token_counts)
    return update(
        norm,
        (att_param, att_moment, att_second, att_grad),
        (exp_param, exp_moment, exp_second, exp_grad),
    )


def solution(mesh):
    in_specs = (
        P("dp", "expert"),
        P("dp", None),
        P("expert", "dp"),
        P("expert", "dp"),
        P("dp", "expert"),
        P("dp", "expert"),
        P("dp", "expert"),
        P("dp", "expert"),
        P(("dp", "expert"), None),
        P(("dp", "expert"), None),
        P(("dp", "expert"), None),
    )
    out_specs = (
        P("dp", "expert"),
        P("dp", "expert"),
        P("dp", "expert"),
        P(("dp", "expert"), None),
        P(("dp", "expert"), None),
        P(("dp", "expert"), None),
    )
    return jax.shard_map(
        on_device, mesh=mesh, in_specs=in_specs, out_specs=out_specs, check_vma=False
    )
```

```python
import functools

import jax
import jax.numpy as jnp
from jax import lax
from jax.experimental import pallas as pl
from jax.experimental.pallas import tpu as pltpu
from jax.sharding import PartitionSpec as P

D = 4096
KV2 = 1024
FF = 1536
DW = 2048
GROUP = 8

beta_one = 0.9
beta_two = 0.95
learn_rate = 0.01
decay_rate = 0.1
epsilon = 1e-08
step_number = 5

NX, NY, NZ, NC = 4, 8, 8, 2
TOK = 384
HID = 192
OWN = HID // NZ
HALVES = 2
SPLIT = 2
PIECES = HALVES * SPLIT
WIDE = DW // PIECES
DEPTH = NZ // 2
COLS = 512
HALF = COLS // 2
ROWS = 16
GROUPS = 4
Y_ORDER = (4, 3, 5, 2, 6, 1, 7, 0)
MESH = pl.DeviceIdType.MESH
BETWEEN = {
    3: (("second", 0),),
    5: (("second", 1),),
    6: (("second", 2),),
    8: (("second", 3), ("third", 0)),
    9: (("third", 1),),
    10: (("third", 2),),
    11: (("third", 3),),
    12: (("last", 0),),
}


def adam_update(param, moment, second, grad, clip):
    scaled = clip * grad
    new_moment = beta_one * moment + (1.0 - beta_one) * scaled
    new_second = beta_two * second + (1.0 - beta_two) * scaled * scaled
    fix_one = 1.0 - beta_one**step_number
    fix_two = 1.0 - beta_two**step_number
    update = new_moment / fix_one / (jnp.sqrt(new_second / fix_two) + epsilon)
    new_param = param - learn_rate * (update + decay_rate * param)
    return (new_param, new_moment, new_second)


def grads_kernel(
    hidden_hbm, cot_hbm, kv_hbm, x_hbm, count_hbm,
    exp_hbm, att_hbm, norm_ref,
    exp_ref, att_ref, count_ref, hidden, cot, kv, xin, masked, part, ring, grad, core_in, keep, send_a, recv_a, keep_b, send_b, recv_b, y_out, y_in,
    norm_c, norm_z, norm_p,
    load_sem, ring_send, ring_recv, core_send, core_recv, a_send, a_recv, b_send, b_recv, y_send, y_recv, norm_send, norm_recv, out_sem,
):
    dp = lax.axis_index("dp")
    z = lax.axis_index("expert")
    c = lax.rem(dp, NC)
    x = lax.rem(dp // NC, NX)
    y = dp // (NC * NX)

    def at(zz, yy, xx, cc):
        return ((yy * NX + xx) * NC + cc, zz)

    x_rel = (x, x + 1 - 2 * lax.rem(x, 2), lax.rem(x + 2, NX), NX - 1 - x)

    barrier = pltpu.get_barrier_semaphore()
    greeted = [at(lax.rem(z + 1, NZ), y, x, c), at(lax.rem(z + NZ - 1, NZ), y, x, c), at(z, y, x, 1 - c)]
    greeted += [at(z, y, x_rel[1], c), at(z, y, x_rel[3], c)]
    greeted += [at(z, lax.rem(y + d, NY), x, c) for d in range(1, NY)]
    for device in greeted:
        pl.semaphore_signal(barrier, inc=1, device_id=device, device_id_type=MESH)

    loads = [pltpu.make_async_copy(hidden_hbm, hidden, load_sem.at[0])]
    for k in range(PIECES):
        loads.append(pltpu.make_async_copy(cot_hbm.at[:, pl.ds(k * WIDE, WIDE)], cot.at[k], load_sem.at[1 + k]))
    loads.append(pltpu.make_async_copy(x_hbm, xin, load_sem.at[1 + PIECES]))
    loads.append(pltpu.make_async_copy(kv_hbm, kv, load_sem.at[2 + PIECES]))
    count_load = pltpu.make_async_copy(count_hbm, count_ref, load_sem.at[3 + PIECES])
    count_load.start()
    for load in loads:
        load.start()

    def squares_of(value):
        rows, width = value.shape
        value = value * value
        total = value[0:8, 0:128]
        for i in range(0, rows, 8):
            for j in range(0, width, 128):
                if i or j:
                    total = total + value[i : i + 8, j : j + 128]
        return total

    sends = []

    def remote(src, dst, send_sem, recv_sem, device):
        copy = pltpu.make_async_remote_copy(
            src_ref=src, dst_ref=dst, send_sem=send_sem, recv_sem=recv_sem, device_id=device, device_id_type=MESH
        )
        copy.start()
        sends.append(copy)
        return copy

    towards = (at(lax.rem(z + NZ - 1, NZ), y, x, c), at(lax.rem(z + 1, NZ), y, x, c))

    def shard(way, hops):
        return lax.rem(z + NZ - hops, NZ) if way == 0 else lax.rem(z + hops, NZ)

    arrivals = {}

    def ring_send_step(way, k, hops, src):
        arrivals[way, k, hops] = remote(
            src, ring.at[way, k, hops - 1], ring_send.at[way, k, hops - 1], ring_recv.at[way, k, hops - 1], towards[way]
        )

    def ring_start(way, k):
        hops = DEPTH if k // SPLIT == way else DEPTH - 1
        ring_send_step(way, k, hops, part.at[k, shard(way, hops)])

    squares, outs = [], []

    def ring_step(way, k, hops):
        arrivals[way, k, hops].wait_recv()
        left = hops - 1
        if left:
            ring[way, k, left] = ring[way, k, left] + part[k, shard(way, left)]
            ring_send_step(way, k, left, ring.at[way, k, left])
            return
        cols = pl.ds(k % PIECES * WIDE, WIDE)
        if k // SPLIT != way:
            exp_ref[:, cols] = part[k, z] + ring[way, k, 0]
        else:
            total = exp_ref[:, cols] + ring[way, k, 0]
            exp_ref[:, cols] = total
            outs.append(pltpu.make_async_copy(exp_ref.at[:, cols], exp_hbm.at[:, cols], out_sem.at[1 + k]))
            outs[-1].start()
            squares.append(squares_of(total))

    count_load.wait()
    loads[0].wait()
    live = lax.broadcasted_iota(jnp.int32, (HID, TOK), 1) < count_ref[0, 0]
    masked[...] = jnp.where(live, hidden[...].astype(jnp.float32), 0.0).astype(jnp.bfloat16)

    def exp_piece(k):
        loads[1 + k].wait()
        block = lax.dot_general(
            masked[...], cot[k], (((1,), (0,)), ((), ())), preferred_element_type=jnp.float32
        )
        part[k] = block.reshape(NZ, OWN, WIDE)

    core_copy, a_copy, b_copy = {}, {}, {}

    def att_group(g):
        if g == 0:
            loads[1 + PIECES].wait()
            loads[2 + PIECES].wait()
        for i in (2 * g, 2 * g + 1):
            target = lax.rem(y + Y_ORDER[i], NY)
            columns = kv[:, pl.ds(pl.multiple_of(target * (KV2 // NY), KV2 // NY), KV2 // NY)]
            block = lax.dot_general(columns, xin[...], (((0,), (0,)), ((), ())), preferred_element_type=jnp.float32)
            grad[i] = block.reshape(NX, NC, ROWS, COLS)
        core_copy[g] = remote(
            grad.at[pl.ds(2 * g, 2), :, 1 - c], core_in.at[g], core_send.at[g], core_recv.at[g], at(z, y, x, 1 - c)
        )

    slots = ((0, 3, 1, 2), (0, 1, 3, 2))
    first_to = (x_rel[1], x_rel[3])
    second_to = (x_rel[3], x_rel[1])

    def att_first(g):
        core_copy[g].wait_recv()
        for h in range(2):
            cols = pl.ds(h * HALF, HALF)
            for j in (2, 3):
                at_x = x_rel[slots[h][j]]
                for i in range(2):
                    send_a[g, h, j - 2, i] = grad[2 * g + i, at_x, c, :, cols] + core_in[g, i, at_x, :, cols]
            a_copy[g, h] = remote(
                send_a.at[g, h], recv_a.at[g, h], a_send.at[g, h], a_recv.at[g, h], at(z, y, first_to[h], c)
            )
        for h in range(2):
            cols = pl.ds(h * HALF, HALF)
            for j in (0, 1):
                at_x = x_rel[slots[h][j]]
                for i in range(2):
                    keep[g, h, j, i] = grad[2 * g + i, at_x, c, :, cols] + core_in[g, i, at_x, :, cols]

    def att_second(g):
        for h in range(2):
            a_copy[g, h].wait_recv()
            send_b[g, h] = keep[g, h, 1] + recv_a[g, h, 1]
            b_copy[g, h] = remote(
                send_b.at[g, h], recv_b.at[g, h], b_send.at[g, h], b_recv.at[g, h], at(z, y, second_to[h], c)
            )
            keep_b[g, h] = keep[g, h, 0] + recv_a[g, h, 0]

    y_copy = {}

    def att_third(g):
        for h in range(2):
            b_copy[g, h].wait_recv()
            for i in range(2):
                y_out[2 * g + i, :, pl.ds(h * HALF, HALF)] = keep_b[g, h, i] + recv_b[g, h, i]
        for i in (2 * g, 2 * g + 1):
            d = Y_ORDER[i]
            if d:
                y_copy[d] = remote(
                    y_out.at[i], y_in.at[d - 1], y_send.at[d - 1], y_recv.at[d - 1], at(z, lax.rem(y + d, NY), x, c)
                )

    def att_last():
        total = y_out[Y_ORDER.index(0)]
        for d in Y_ORDER:
            if d:
                y_copy[d].wait_recv()
                total = total + y_in[d - 1]
        att_ref[...] = total
        outs.append(pltpu.make_async_copy(att_ref, att_hbm, out_sem.at[0]))
        outs[-1].start()
        squares.append(squares_of(total))

    work = {"second": att_second, "third": att_third, "last": lambda g: att_last()}

    for n in range(PIECES):
        way, k = n % 2, n % 2 * SPLIT + n // 2
        exp_piece(k)
        if n == 0:
            pl.semaphore_wait(barrier, len(greeted))
        ring_start(way, k)
        if n == 1:
            att_group(0)
    for n in range(PIECES):
        way, k = n % 2, (1 - n % 2) * SPLIT + n // 2
        ring_start(way, k)
    for g in range(1, GROUPS):
        att_group(g)
    for g in range(GROUPS):
        att_first(g)
    event = 0
    for unit in range(2 * DEPTH - 1):
        hops = DEPTH - (unit + 1) // 2
        for p in range(SPLIT):
            for way in range(2):
                half = way if unit % 2 == 0 else 1 - way
                ring_step(way, half * SPLIT + p, hops)
            for name, g in BETWEEN.get(event * 2 // SPLIT, ()) if event * 2 % SPLIT == 0 else ():
                work[name](g)
            event += 1

    value = squares[0]
    for other in squares[1:]:
        value = value + other
    norm_c[...] = jnp.sum(value, axis=0, keepdims=True)

    def norm_copy(n, src, dst, device):
        return pltpu.make_async_remote_copy(
            src_ref=src, dst_ref=dst, send_sem=norm_send.at[n], recv_sem=norm_recv.at[n],
            device_id=device, device_id_type=MESH,
        )

    for d in (4, 3, 5, 2, 6, 1, 7):
        norm_copy(0, norm_c, norm_z.at[d * NC + c], at(lax.rem(z + d, NZ), y, x, 1)).start()

    @pl.when(c == 0)
    def _():
        norm_copy(0, norm_c, norm_z.at[0], at(z, y, x, 1)).start()

    for copy in sends:
        copy.wait_send()
    for out in outs:
        out.wait()

    @pl.when(c == 0)
    def _():
        sent = norm_z.at[pl.ds(0, NZ)]
        pltpu.make_async_copy(sent, sent, norm_send.at[0]).wait()
        pltpu.make_async_copy(norm_p, norm_p, norm_recv.at[1]).wait()

    @pl.when(c == 1)
    def _():
        norm_z[1] = norm_c[...]
        others = norm_z.at[pl.ds(0, NZ * NC - 1)]
        pltpu.make_async_copy(others, others, norm_recv.at[0]).wait()
        norm_p[0] = jnp.sum(norm_z[...], axis=0)
        plane = [(dy, dx) for dy in range(NY) for dx in range(NX) if dy or dx]
        plane.sort(key=lambda e: -min(e[0], NY - e[0]) - min(e[1], NX - e[1]))
        for core in range(NC):
            for dy, dx in plane if core else plane + [(0, 0)]:
                device = at(z, lax.rem(y + dy, NY), lax.rem(x + dx, NX), core)
                norm_copy(1, norm_p.at[0], norm_p.at[dy * NX + dx], device).start()
        sent = norm_z.at[pl.ds(0, NZ - 1)]
        pltpu.make_async_copy(sent, sent, norm_send.at[0]).wait()
        others = norm_p.at[pl.ds(1, NX * NY - 1)]
        pltpu.make_async_copy(others, others, norm_recv.at[1]).wait()
        for sent in (norm_p, others):
            pltpu.make_async_copy(sent, sent, norm_send.at[1]).wait()

    norm_ref[...] = jnp.sum(norm_p[...], axis=0)


def grads(hidden, cot, kv, xin, counts):
    f32, bf16 = jnp.float32, jnp.bfloat16
    dma = pltpu.SemaphoreType.DMA
    hbm = pl.BlockSpec(memory_space=pltpu.HBM)
    vmem = pl.BlockSpec(memory_space=pltpu.VMEM)
    return pl.pallas_call(
        grads_kernel,
        out_shape=tuple(jax.ShapeDtypeStruct(shape, f32) for shape in ((OWN, DW), (ROWS, COLS), (1, 128))),
        in_specs=[hbm] * 5,
        out_specs=(hbm, hbm, vmem),
        scratch_shapes=[
            pltpu.VMEM((OWN, DW), f32),
            pltpu.VMEM((ROWS, COLS), f32),
            pltpu.SMEM((1, 1), jnp.int32),
            pltpu.VMEM((HID, TOK), bf16),
            pltpu.VMEM((PIECES, TOK, WIDE), bf16),
            pltpu.VMEM((TOK, KV2), bf16),
            pltpu.VMEM((TOK, COLS), bf16),
            pltpu.VMEM((HID, TOK), bf16),
            pltpu.VMEM((PIECES, NZ, OWN, WIDE), f32),
            pltpu.VMEM((2, PIECES, DEPTH, OWN, WIDE), f32),
            pltpu.VMEM((NY, NX, NC, ROWS, COLS), f32),
            pltpu.VMEM((GROUPS, 2, NX, ROWS, COLS), f32),
            pltpu.VMEM((GROUPS, 2, 2, 2, ROWS, HALF), f32),
            pltpu.VMEM((GROUPS, 2, 2, 2, ROWS, HALF), f32),
            pltpu.VMEM((GROUPS, 2, 2, 2, ROWS, HALF), f32),
            pltpu.VMEM((GROUPS, 2, 2, ROWS, HALF), f32),
            pltpu.VMEM((GROUPS, 2, 2, ROWS, HALF), f32),
            pltpu.VMEM((GROUPS, 2, 2, ROWS, HALF), f32),
            pltpu.VMEM((NY, ROWS, COLS), f32),
            pltpu.VMEM((NY - 1, ROWS, COLS), f32),
            pltpu.VMEM((1, 128), f32),
            pltpu.VMEM((NZ * NC, 1, 128), f32),
            pltpu.VMEM((NX * NY, 1, 128), f32),
            dma((4 + PIECES,)),
            dma((2, PIECES, DEPTH)),
            dma((2, PIECES, DEPTH)),
            dma((GROUPS,)),
            dma((GROUPS,)),
            dma((GROUPS, 2)),
            dma((GROUPS, 2)),
            dma((GROUPS, 2)),
            dma((GROUPS, 2)),
            dma((NY - 1,)),
            dma((NY - 1,)),
            dma((2,)),
            dma((2,)),
            dma((1 + PIECES,)),
        ],
        compiler_params=pltpu.CompilerParams(
            collective_id=0, has_side_effects=True, vmem_limit_bytes=60 * 1024 * 1024
        ),
        name="grads",
    )(hidden, cot, kv, xin, counts)


BLOCKS = 4


def update_kernel(norm_hbm, *refs):
    att_in, exp_in, att_out, exp_out = refs[0:4], refs[4:8], refs[8:11], refs[11:14]
    norm, att, exp, new_att, new_exp, load_sem, store_sem = refs[14:]
    wide = DW // BLOCKS
    cols = [pl.ds(n * wide, wide) for n in range(BLOCKS)]
    loads = [[pltpu.make_async_copy(norm_hbm, norm, load_sem.at[0, 4])]]
    loads[0] += [pltpu.make_async_copy(a, att.at[i], load_sem.at[0, i]) for i, a in enumerate(att_in)]
    for n in range(BLOCKS):
        loads.append(
            [pltpu.make_async_copy(a.at[:, cols[n]], exp.at[i, :, cols[n]], load_sem.at[1 + n, i]) for i, a in enumerate(exp_in)]
        )
    for part in loads:
        for load in part:
            load.start()
    stores = []

    def block(n, values, keep, sources, targets):
        new = adam_update(*values, clip)
        for i in range(3):
            keep(i, new[i])
            stores.append(pltpu.make_async_copy(sources[i], targets[i], store_sem.at[n, i]))
            stores[-1].start()

    for load in loads[0]:
        load.wait()
    entries = float(KV2 * D + NY * NX * NC // GROUP * FF * DW)
    square_sum = jnp.sum(norm[...], axis=1, keepdims=True)
    clip = jnp.minimum(1.0, jnp.sqrt(jnp.full_like(square_sum, entries)) / (jnp.sqrt(square_sum) + 1e-06))

    def keep_att(i, value):
        new_att[i] = value

    block(0, [att[i] for i in range(4)], keep_att, [new_att.at[i] for i in range(3)], att_out)
    for n in range(BLOCKS):
        for load in loads[1 + n]:
            load.wait()

        def keep_exp(i, value):
            new_exp[i, :, cols[n]] = value

        block(
            1 + n,
            [exp[i, :, cols[n]] for i in range(4)],
            keep_exp,
            [new_exp.at[i, :, cols[n]] for i in range(3)],
            [ref.at[:, cols[n]] for ref in exp_out],
        )
    for store in stores:
        store.wait()


def update(norm, att, exp):
    f32 = jnp.float32
    hbm = pl.BlockSpec(memory_space=pltpu.HBM)
    return pl.pallas_call(
        update_kernel,
        out_shape=tuple(jax.ShapeDtypeStruct(a.shape, f32) for a in (*att[:3], *exp[:3])),
        in_specs=[hbm] * 9,
        out_specs=(hbm,) * 6,
        scratch_shapes=[
            pltpu.VMEM((1, 128), f32),
            pltpu.VMEM((4, ROWS, COLS), f32),
            pltpu.VMEM((4, OWN, DW), f32),
            pltpu.VMEM((3, ROWS, COLS), f32),
            pltpu.VMEM((3, OWN, DW), f32),
            pltpu.SemaphoreType.DMA((1 + BLOCKS, 5)),
            pltpu.SemaphoreType.DMA((1 + BLOCKS, 3)),
        ],
        compiler_params=pltpu.CompilerParams(vmem_limit_bytes=60 * 1024 * 1024),
        name="update",
    )(norm, *att, *exp)


def on_device(
    att_input,
    kv_cotangent,
    expert_hidden,
    expert_cotangent,
    token_counts,
    att_param,
    att_moment,
    att_second,
    exp_param,
    exp_moment,
    exp_second,
):
    exp_grad, att_grad, norm = grads(expert_hidden.T, expert_cotangent, kv_cotangent, att_input, token_counts)
    return update(
        norm,
        (att_param, att_moment, att_second, att_grad),
        (exp_param, exp_moment, exp_second, exp_grad),
    )


def solution(mesh):
    in_specs = (
        P("dp", "expert"),
        P("dp", None),
        P("expert", "dp"),
        P("expert", "dp"),
        P("dp", "expert"),
        P("dp", "expert"),
        P("dp", "expert"),
        P("dp", "expert"),
        P(("dp", "expert"), None),
        P(("dp", "expert"), None),
        P(("dp", "expert"), None),
    )
    out_specs = (
        P("dp", "expert"),
        P("dp", "expert"),
        P("dp", "expert"),
        P(("dp", "expert"), None),
        P(("dp", "expert"), None),
        P(("dp", "expert"), None),
    )
    return jax.shard_map(
        on_device, mesh=mesh, in_specs=in_specs, out_specs=out_specs, check_vma=False
    )
```

```python
import functools

import jax
import jax.numpy as jnp
from jax import lax
from jax.experimental import pallas as pl
from jax.experimental.pallas import tpu as pltpu
from jax.sharding import PartitionSpec as P

D = 4096
KV2 = 1024
FF = 1536
DW = 2048
GROUP = 8

beta_one = 0.9
beta_two = 0.95
learn_rate = 0.01
decay_rate = 0.1
epsilon = 1e-08
step_number = 5

NX, NY, NZ, NC = 4, 8, 8, 2
TOK = 384
HID = 192
OWN = HID // NZ
HALVES = 2
SPLIT = 2
PIECES = HALVES * SPLIT
WIDE = DW // PIECES
DEPTH = NZ // 2
SLOTS = {}
for _way in range(2):
    for _piece in range(PIECES):
        for _hops in range(1, DEPTH + (_piece // SPLIT == _way)):
            SLOTS[_way, _piece, _hops] = len(SLOTS)
COLS = 512
HALF = COLS // 2
ROWS = 16
GROUPS = 4
Y_ORDER = (4, 3, 5, 2, 6, 1, 7, 0)
MESH = pl.DeviceIdType.MESH
RING, ATT, NORM = True, True, True
BETWEEN = {
    1: (('second', 0),),
    2: (('second', 1),),
    3: (('second', 2),),
    5: (('second', 3), ('third', 0)),
    6: (('third', 1),),
    7: (('third', 2),),
    8: (('third', 3),),
    11: (('last', 0),),
}


def adam_update(param, moment, second, grad, clip):
    scaled = clip * grad
    new_moment = beta_one * moment + (1.0 - beta_one) * scaled
    new_second = beta_two * second + (1.0 - beta_two) * scaled * scaled
    fix_one = 1.0 - beta_one**step_number
    fix_two = 1.0 - beta_two**step_number
    update = new_moment / fix_one / (jnp.sqrt(new_second / fix_two) + epsilon)
    new_param = param - learn_rate * (update + decay_rate * param)
    return (new_param, new_moment, new_second)


def grads_kernel(
    hidden_hbm, cot_hbm, kv_hbm, x_hbm, count_hbm,
    exp_hbm, att_hbm, norm_ref,
    exp_ref, att_ref, count_ref, hidden, cot, kv, xin, masked, part, ring, grad, core_in, keep, send_a, recv_a, keep_b, send_b, recv_b, y_out, y_in,
    norm_c, norm_z, norm_p,
    load_sem, ring_send, ring_recv, core_send, core_recv, a_send, a_recv, b_send, b_recv, y_send, y_recv, norm_send, norm_recv, out_sem,
):
    dp = lax.axis_index("dp")
    z = lax.axis_index("expert")
    c = lax.rem(dp, NC)
    x = lax.rem(dp // NC, NX)
    y = dp // (NC * NX)

    def at(zz, yy, xx, cc):
        return ((yy * NX + xx) * NC + cc, zz)

    x_rel = (x, x + 1 - 2 * lax.rem(x, 2), lax.rem(x + 2, NX), NX - 1 - x)

    barrier = pltpu.get_barrier_semaphore()
    greeted = [at(lax.rem(z + 1, NZ), y, x, c), at(lax.rem(z + NZ - 1, NZ), y, x, c), at(z, y, x, 1 - c)]
    greeted += [at(z, y, x_rel[1], c), at(z, y, x_rel[3], c)]
    greeted += [at(z, lax.rem(y + d, NY), x, c) for d in range(1, NY)]
    for device in greeted:
        pl.semaphore_signal(barrier, inc=1, device_id=device, device_id_type=MESH)

    loads = [pltpu.make_async_copy(hidden_hbm, hidden, load_sem.at[0])]
    for k in range(PIECES):
        loads.append(pltpu.make_async_copy(cot_hbm.at[:, pl.ds(k * WIDE, WIDE)], cot.at[k], load_sem.at[1 + k]))
    loads.append(pltpu.make_async_copy(x_hbm, xin, load_sem.at[1 + PIECES]))
    loads.append(pltpu.make_async_copy(kv_hbm, kv, load_sem.at[2 + PIECES]))
    count_load = pltpu.make_async_copy(count_hbm, count_ref, load_sem.at[3 + PIECES])
    count_load.start()
    for load in loads:
        load.start()

    def squares_of(value):
        rows, width = value.shape
        value = value * value
        total = value[0:8, 0:128]
        for i in range(0, rows, 8):
            for j in range(0, width, 128):
                if i or j:
                    total = total + value[i : i + 8, j : j + 128]
        return total

    def arrived(ref, sem):
        pltpu.make_async_copy(ref, ref, sem).wait()

    def remote(src, dst, send_sem, recv_sem, device):
        copy = pltpu.make_async_remote_copy(
            src_ref=src, dst_ref=dst, send_sem=send_sem, recv_sem=recv_sem, device_id=device, device_id_type=MESH
        )
        copy.start()
        return copy

    towards = (at(lax.rem(z + NZ - 1, NZ), y, x, c), at(lax.rem(z + 1, NZ), y, x, c))

    def shard(way, hops):
        return lax.rem(z + NZ - hops, NZ) if way == 0 else lax.rem(z + hops, NZ)

    arrivals = {}

    def ring_send_step(way, k, hops, src):
        if not RING:
            return
        slot = SLOTS[way, k, hops]
        arrivals[way, k, hops] = remote(src, ring.at[slot], ring_send.at[0], ring_recv.at[slot], towards[way])

    def ring_start(way, k):
        if not RING:
            return
        hops = DEPTH if k // SPLIT == way else DEPTH - 1
        ring_send_step(way, k, hops, part.at[k, shard(way, hops)])

    squares = []

    def ring_step(way, k, hops):
        if RING:
            arrivals[way, k, hops].wait_recv()
        left = hops - 1
        slot = SLOTS[way, k, hops]
        if left:
            ring[slot] = ring[slot] + part[k, shard(way, left)]
            ring_send_step(way, k, left, ring.at[slot])
            return
        cols = pl.ds(k % PIECES * WIDE, WIDE)
        if k // SPLIT != way:
            exp_ref[:, cols] = part[k, z] + ring[slot]
        else:
            total = exp_ref[:, cols] + ring[slot]
            exp_ref[:, cols] = total
            pltpu.make_async_copy(exp_ref.at[:, cols], exp_hbm.at[:, cols], out_sem.at[0]).start()
            squares.append(squares_of(total))

    count_load.wait()
    loads[0].wait()
    live = lax.broadcasted_iota(jnp.int32, (HID, TOK), 1) < count_ref[0, 0]
    masked[...] = jnp.where(live, hidden[...].astype(jnp.float32), 0.0).astype(jnp.bfloat16)

    def exp_piece(k):
        loads[1 + k].wait()
        block = lax.dot_general(
            masked[...], cot[k], (((1,), (0,)), ((), ())), preferred_element_type=jnp.float32
        )
        part[k] = block.reshape(NZ, OWN, WIDE)

    core_copy = {}

    def att_group(g):
        if not ATT:
            return
        if g == 0:
            loads[1 + PIECES].wait()
            loads[2 + PIECES].wait()
        for i in (2 * g, 2 * g + 1):
            target = lax.rem(y + Y_ORDER[i], NY)
            columns = kv[:, pl.ds(pl.multiple_of(target * (KV2 // NY), KV2 // NY), KV2 // NY)]
            block = lax.dot_general(columns, xin[...], (((0,), (0,)), ((), ())), preferred_element_type=jnp.float32)
            grad[i] = block.reshape(NX, NC, ROWS, COLS)
        core_copy[g] = remote(
            grad.at[pl.ds(2 * g, 2), :, 1 - c], core_in.at[g], core_send.at[0], core_recv.at[g], at(z, y, x, 1 - c)
        )

    slots = ((0, 3, 1, 2), (0, 1, 3, 2))
    first_to = (x_rel[1], x_rel[3])
    second_to = (x_rel[3], x_rel[1])

    def att_first(g):
        if not ATT:
            return
        core_copy[g].wait_recv()
        for h in range(2):
            cols = pl.ds(h * HALF, HALF)
            for j in (2, 3):
                at_x = x_rel[slots[h][j]]
                for i in range(2):
                    send_a[g, h, j - 2, i] = grad[2 * g + i, at_x, c, :, cols] + core_in[g, i, at_x, :, cols]
            remote(
                send_a.at[g, h], recv_a.at[g, h], a_send.at[0], a_recv.at[g], at(z, y, first_to[h], c)
            )
        for h in range(2):
            cols = pl.ds(h * HALF, HALF)
            for j in (0, 1):
                at_x = x_rel[slots[h][j]]
                for i in range(2):
                    keep[g, h, j, i] = grad[2 * g + i, at_x, c, :, cols] + core_in[g, i, at_x, :, cols]

    def att_second(g):
        if not ATT:
            return
        arrived(recv_a.at[g], a_recv.at[g])
        for h in range(2):
            send_b[g, h] = keep[g, h, 1] + recv_a[g, h, 1]
            remote(
                send_b.at[g, h], recv_b.at[g, h], b_send.at[0], b_recv.at[g], at(z, y, second_to[h], c)
            )
            keep_b[g, h] = keep[g, h, 0] + recv_a[g, h, 0]

    def att_third(g):
        if not ATT:
            return
        arrived(recv_b.at[g], b_recv.at[g])
        for h in range(2):
            for i in range(2):
                y_out[2 * g + i, :, pl.ds(h * HALF, HALF)] = keep_b[g, h, i] + recv_b[g, h, i]
        for i in (2 * g, 2 * g + 1):
            d = Y_ORDER[i]
            if d:
                remote(
                    y_out.at[i], y_in.at[d - 1], y_send.at[0], y_recv.at[0], at(z, lax.rem(y + d, NY), x, c)
                )

    def att_last():
        if not ATT:
            return
        arrived(y_in, y_recv.at[0])
        total = y_out[Y_ORDER.index(0)]
        for d in Y_ORDER:
            if d:
                total = total + y_in[d - 1]
        att_ref[...] = total
        pltpu.make_async_copy(att_ref, att_hbm, out_sem.at[1]).start()
        squares.append(squares_of(total))

    work = {"second": att_second, "third": att_third, "last": lambda g: att_last()}

    for n in range(PIECES):
        way, k = n % 2, n % 2 * SPLIT + n // 2
        exp_piece(k)
        if n == 0:
            pl.semaphore_wait(barrier, len(greeted))
        ring_start(way, k)
        if n == 1:
            att_group(0)
    for n in range(PIECES):
        way, k = n % 2, (1 - n % 2) * SPLIT + n // 2
        ring_start(way, k)
    for g in range(1, GROUPS):
        att_group(g)
    for g in range(GROUPS):
        att_first(g)
    event = 0
    for unit in range(2 * DEPTH - 1):
        hops = DEPTH - (unit + 1) // 2
        for p in range(SPLIT):
            for way in range(2):
                half = way if unit % 2 == 0 else 1 - way
                ring_step(way, half * SPLIT + p, hops)
            for name, g in BETWEEN.get(event * 2 // SPLIT, ()) if event * 2 % SPLIT == 0 else ():
                work[name](g)
            event += 1

    value = squares[0]
    for other in squares[1:]:
        value = value + other
    norm_c[...] = jnp.sum(value, axis=0, keepdims=True)

    def norm_copy(n, src, dst, device):
        return pltpu.make_async_remote_copy(
            src_ref=src, dst_ref=dst, send_sem=norm_send.at[n], recv_sem=norm_recv.at[n],
            device_id=device, device_id_type=MESH,
        )

    for d in (4, 3, 5, 2, 6, 1, 7):
        norm_copy(0, norm_c, norm_z.at[d * NC + c], at(lax.rem(z + d, NZ), y, x, 1)).start()

    @pl.when(c == 0)
    def _():
        norm_copy(0, norm_c, norm_z.at[0], at(z, y, x, 1)).start()

    for ref, sem in (
        (ring, ring_send), (core_in, core_send), (send_a, a_send), (send_b, b_send), (y_in, y_send), (exp_ref, out_sem)
    ):
        arrived(ref, sem.at[0])
    arrived(att_ref, out_sem.at[1])

    @pl.when(c == 0)
    def _():
        sent = norm_z.at[pl.ds(0, NZ)]
        pltpu.make_async_copy(sent, sent, norm_send.at[0]).wait()
        pltpu.make_async_copy(norm_p, norm_p, norm_recv.at[1]).wait()

    @pl.when(c == 1)
    def _():
        norm_z[1] = norm_c[...]
        others = norm_z.at[pl.ds(0, NZ * NC - 1)]
        pltpu.make_async_copy(others, others, norm_recv.at[0]).wait()
        norm_p[0] = jnp.sum(norm_z[...], axis=0)
        plane = [(dy, dx) for dy in range(NY) for dx in range(NX) if dy or dx]
        plane.sort(key=lambda e: -min(e[0], NY - e[0]) - min(e[1], NX - e[1]))
        for core in range(NC):
            for dy, dx in plane if core else plane + [(0, 0)]:
                device = at(z, lax.rem(y + dy, NY), lax.rem(x + dx, NX), core)
                norm_copy(1, norm_p.at[0], norm_p.at[dy * NX + dx], device).start()
        sent = norm_z.at[pl.ds(0, NZ - 1)]
        pltpu.make_async_copy(sent, sent, norm_send.at[0]).wait()
        others = norm_p.at[pl.ds(1, NX * NY - 1)]
        pltpu.make_async_copy(others, others, norm_recv.at[1]).wait()
        for sent in (norm_p, others):
            pltpu.make_async_copy(sent, sent, norm_send.at[1]).wait()

    norm_ref[...] = jnp.sum(norm_p[...], axis=0)


def grads(hidden, cot, kv, xin, counts):
    f32, bf16 = jnp.float32, jnp.bfloat16
    dma = pltpu.SemaphoreType.DMA
    hbm = pl.BlockSpec(memory_space=pltpu.HBM)
    vmem = pl.BlockSpec(memory_space=pltpu.VMEM)
    return pl.pallas_call(
        grads_kernel,
        out_shape=tuple(jax.ShapeDtypeStruct(shape, f32) for shape in ((OWN, DW), (ROWS, COLS), (1, 128))),
        in_specs=[hbm] * 5,
        out_specs=(hbm, hbm, vmem),
        scratch_shapes=[
            pltpu.VMEM((OWN, DW), f32),
            pltpu.VMEM((ROWS, COLS), f32),
            pltpu.SMEM((1, 1), jnp.int32),
            pltpu.VMEM((HID, TOK), bf16),
            pltpu.VMEM((PIECES, TOK, WIDE), bf16),
            pltpu.VMEM((TOK, KV2), bf16),
            pltpu.VMEM((TOK, COLS), bf16),
            pltpu.VMEM((HID, TOK), bf16),
            pltpu.VMEM((PIECES, NZ, OWN, WIDE), f32),
            pltpu.VMEM((len(SLOTS), OWN, WIDE), f32),
            pltpu.VMEM((NY, NX, NC, ROWS, COLS), f32),
            pltpu.VMEM((GROUPS, 2, NX, ROWS, COLS), f32),
            pltpu.VMEM((GROUPS, 2, 2, 2, ROWS, HALF), f32),
            pltpu.VMEM((GROUPS, 2, 2, 2, ROWS, HALF), f32),
            pltpu.VMEM((GROUPS, 2, 2, 2, ROWS, HALF), f32),
            pltpu.VMEM((GROUPS, 2, 2, ROWS, HALF), f32),
            pltpu.VMEM((GROUPS, 2, 2, ROWS, HALF), f32),
            pltpu.VMEM((GROUPS, 2, 2, ROWS, HALF), f32),
            pltpu.VMEM((NY, ROWS, COLS), f32),
            pltpu.VMEM((NY - 1, ROWS, COLS), f32),
            pltpu.VMEM((1, 128), f32),
            pltpu.VMEM((NZ * NC, 1, 128), f32),
            pltpu.VMEM((NX * NY, 1, 128), f32),
            dma((4 + PIECES,)),
            dma((1,)),
            dma((len(SLOTS),)),
            dma((1,)),
            dma((GROUPS,)),
            dma((1,)),
            dma((GROUPS,)),
            dma((1,)),
            dma((GROUPS,)),
            dma((1,)),
            dma((1,)),
            dma((2,)),
            dma((2,)),
            dma((2,)),
        ],
        compiler_params=pltpu.CompilerParams(
            collective_id=0, has_side_effects=True, vmem_limit_bytes=55091 * 1024
        ),
        name="grads",
    )(hidden, cot, kv, xin, counts)


BLOCKS = 4


def update_kernel(norm_hbm, *refs):
    att_in, exp_in, att_out, exp_out = refs[0:4], refs[4:8], refs[8:11], refs[11:14]
    norm, att, exp, new_att, new_exp, load_sem, store_sem = refs[14:]
    wide = DW // BLOCKS
    cols = [pl.ds(n * wide, wide) for n in range(BLOCKS)]
    pltpu.make_async_copy(norm_hbm, norm, load_sem.at[0]).start()
    for i, a in enumerate(att_in):
        pltpu.make_async_copy(a, att.at[i], load_sem.at[1]).start()
    for n in range(BLOCKS):
        for i, a in enumerate(exp_in):
            pltpu.make_async_copy(a.at[:, cols[n]], exp.at[i, :, cols[n]], load_sem.at[2 + n]).start()

    def arrived(ref, sem):
        pltpu.make_async_copy(ref, ref, sem).wait()

    def block(values, keep, sources, targets, sem):
        new = adam_update(*values, clip)
        for i in range(3):
            keep(i, new[i])
            pltpu.make_async_copy(sources[i], targets[i], sem).start()

    arrived(norm, load_sem.at[0])
    arrived(att, load_sem.at[1])
    entries = float(KV2 * D + NY * NX * NC // GROUP * FF * DW)
    square_sum = jnp.sum(norm[...], axis=1, keepdims=True)
    clip = jnp.minimum(1.0, jnp.sqrt(jnp.full_like(square_sum, entries)) / (jnp.sqrt(square_sum) + 1e-06))

    def keep_att(i, value):
        new_att[i] = value

    block([att[i] for i in range(4)], keep_att, [new_att.at[i] for i in range(3)], att_out, store_sem.at[0])
    for n in range(BLOCKS):
        arrived(exp.at[:, :, cols[n]], load_sem.at[2 + n])

        def keep_exp(i, value):
            new_exp[i, :, cols[n]] = value

        block(
            [exp[i, :, cols[n]] for i in range(4)],
            keep_exp,
            [new_exp.at[i, :, cols[n]] for i in range(3)],
            [ref.at[:, cols[n]] for ref in exp_out],
            store_sem.at[1],
        )
    arrived(new_att, store_sem.at[0])
    arrived(new_exp, store_sem.at[1])


def update(norm, att, exp):
    f32 = jnp.float32
    hbm = pl.BlockSpec(memory_space=pltpu.HBM)
    return pl.pallas_call(
        update_kernel,
        out_shape=tuple(jax.ShapeDtypeStruct(a.shape, f32) for a in (*att[:3], *exp[:3])),
        in_specs=[hbm] * 9,
        out_specs=(hbm,) * 6,
        scratch_shapes=[
            pltpu.VMEM((1, 128), f32),
            pltpu.VMEM((4, ROWS, COLS), f32),
            pltpu.VMEM((4, OWN, DW), f32),
            pltpu.VMEM((3, ROWS, COLS), f32),
            pltpu.VMEM((3, OWN, DW), f32),
            pltpu.SemaphoreType.DMA((2 + BLOCKS,)),
            pltpu.SemaphoreType.DMA((2,)),
        ],
        compiler_params=pltpu.CompilerParams(vmem_limit_bytes=55091 * 1024),
        name="update",
    )(norm, *att, *exp)


def on_device(
    att_input,
    kv_cotangent,
    expert_hidden,
    expert_cotangent,
    token_counts,
    att_param,
    att_moment,
    att_second,
    exp_param,
    exp_moment,
    exp_second,
):
    exp_grad, att_grad, norm = grads(expert_hidden.T, expert_cotangent, kv_cotangent, att_input, token_counts)
    return update(
        norm,
        (att_param, att_moment, att_second, att_grad),
        (exp_param, exp_moment, exp_second, exp_grad),
    )


def solution(mesh):
    in_specs = (
        P("dp", "expert"),
        P("dp", None),
        P("expert", "dp"),
        P("expert", "dp"),
        P("dp", "expert"),
        P("dp", "expert"),
        P("dp", "expert"),
        P("dp", "expert"),
        P(("dp", "expert"), None),
        P(("dp", "expert"), None),
        P(("dp", "expert"), None),
    )
    out_specs = (
        P("dp", "expert"),
        P("dp", "expert"),
        P("dp", "expert"),
        P(("dp", "expert"), None),
        P(("dp", "expert"), None),
        P(("dp", "expert"), None),
    )
    return jax.shard_map(
        on_device, mesh=mesh, in_specs=in_specs, out_specs=out_specs, check_vma=False
    )
```

```python
import functools

import jax
import jax.numpy as jnp
from jax import lax
from jax.experimental import pallas as pl
from jax.experimental.pallas import tpu as pltpu
from jax.sharding import PartitionSpec as P

D = 4096
KV2 = 1024
FF = 1536
DW = 2048
GROUP = 8

beta_one = 0.9
beta_two = 0.95
learn_rate = 0.01
decay_rate = 0.1
epsilon = 1e-08
step_number = 5

NX, NY, NZ, NC = 4, 8, 8, 2
TOK = 384
HID = 192
OWN = HID // NZ
HALVES = 2
SPLIT = 2
PIECES = HALVES * SPLIT
WIDE = DW // PIECES
DEPTH = NZ // 2
STEPS = [
    (DEPTH - (unit + 1) // 2, unit % 2 * SPLIT + p, (1 - unit % 2) * SPLIT + p)
    for unit in range(2 * DEPTH - 1)
    for p in range(SPLIT)
]
SLOTS = {(way, step[1 + way], step[0]): (n, way) for n, step in enumerate(STEPS) for way in range(2)}
COLS = 512
HALF = COLS // 2
ROWS = 16
GROUPS = 4
Y_ORDER = (4, 3, 5, 2, 6, 1, 7, 0)
MESH = pl.DeviceIdType.MESH
RING, ATT, NORM = True, True, True
BETWEEN = {
    1: (('second', 0),),
    2: (('second', 1),),
    3: (('second', 2),),
    5: (('second', 3), ('third', 0)),
    6: (('third', 1),),
    7: (('third', 2),),
    8: (('third', 3),),
    11: (('last', 0),),
}


def adam_update(param, moment, second, grad, clip):
    scaled = clip * grad
    new_moment = beta_one * moment + (1.0 - beta_one) * scaled
    new_second = beta_two * second + (1.0 - beta_two) * scaled * scaled
    fix_one = 1.0 - beta_one**step_number
    fix_two = 1.0 - beta_two**step_number
    update = new_moment / fix_one / (jnp.sqrt(new_second / fix_two) + epsilon)
    new_param = param - learn_rate * (update + decay_rate * param)
    return (new_param, new_moment, new_second)


def grads_kernel(
    hidden_hbm, cot_hbm, kv_hbm, x_hbm, count_hbm,
    exp_hbm, att_hbm, norm_ref,
    exp_ref, att_ref, count_ref, hidden, cot, kv, xin, masked, part, ring, grad, core_in, keep, send_a, recv_a, keep_b, send_b, recv_b, y_out, y_in,
    norm_c, norm_z, norm_p,
    load_sem, ring_send, ring_recv, core_send, core_recv, a_send, a_recv, b_send, b_recv, y_send, y_recv, norm_send, norm_recv, out_sem,
):
    dp = lax.axis_index("dp")
    z = lax.axis_index("expert")
    c = lax.rem(dp, NC)
    x = lax.rem(dp // NC, NX)
    y = dp // (NC * NX)

    def at(zz, yy, xx, cc):
        return ((yy * NX + xx) * NC + cc, zz)

    x_rel = (x, x + 1 - 2 * lax.rem(x, 2), lax.rem(x + 2, NX), NX - 1 - x)

    barrier = pltpu.get_barrier_semaphore()
    greeted = [at(lax.rem(z + 1, NZ), y, x, c), at(lax.rem(z + NZ - 1, NZ), y, x, c), at(z, y, x, 1 - c)]
    greeted += [at(z, y, x_rel[1], c), at(z, y, x_rel[3], c)]
    greeted += [at(z, lax.rem(y + d, NY), x, c) for d in range(1, NY)]
    for device in greeted:
        pl.semaphore_signal(barrier, inc=1, device_id=device, device_id_type=MESH)

    loads = [pltpu.make_async_copy(hidden_hbm, hidden, load_sem.at[0])]
    for k in range(PIECES):
        loads.append(pltpu.make_async_copy(cot_hbm.at[:, pl.ds(k * WIDE, WIDE)], cot.at[k], load_sem.at[1 + k]))
    loads.append(pltpu.make_async_copy(x_hbm, xin, load_sem.at[1 + PIECES]))
    loads.append(pltpu.make_async_copy(kv_hbm, kv, load_sem.at[2 + PIECES]))
    count_load = pltpu.make_async_copy(count_hbm, count_ref, load_sem.at[3 + PIECES])
    count_load.start()
    for n in (1 + PIECES, 2 + PIECES, *range(1 + PIECES)):
        loads[n].start()

    def squares_of(value):
        rows, width = value.shape
        value = value * value
        total = value[0:8, 0:128]
        for i in range(0, rows, 8):
            for j in range(0, width, 128):
                if i or j:
                    total = total + value[i : i + 8, j : j + 128]
        return total

    def arrived(ref, sem):
        pltpu.make_async_copy(ref, ref, sem).wait()

    def remote(src, dst, send_sem, recv_sem, device):
        copy = pltpu.make_async_remote_copy(
            src_ref=src, dst_ref=dst, send_sem=send_sem, recv_sem=recv_sem, device_id=device, device_id_type=MESH
        )
        copy.start()
        return copy

    towards = (at(lax.rem(z + NZ - 1, NZ), y, x, c), at(lax.rem(z + 1, NZ), y, x, c))

    def shard(way, hops):
        return lax.rem(z + NZ - hops, NZ) if way == 0 else lax.rem(z + hops, NZ)

    def ring_send_step(way, k, hops, src):
        if not RING:
            return
        n, _ = SLOTS[way, k, hops]
        remote(src, ring.at[n, way], ring_send.at[0], ring_recv.at[n], towards[way])

    def ring_start(way, k):
        if not RING:
            return
        hops = DEPTH if k // SPLIT == way else DEPTH - 1
        ring_send_step(way, k, hops, part.at[k, shard(way, hops)])

    squares = []

    def ring_step(n):
        hops, down, up = STEPS[n]
        left = hops - 1
        arrived(ring.at[n], ring_recv.at[n])
        for way, k in enumerate((down, up)):
            if left:
                ring[n, way] = ring[n, way] + part[k, shard(way, left)]
                ring_send_step(way, k, left, ring.at[n, way])
                continue
            cols = pl.ds(k * WIDE, WIDE)
            if k // SPLIT != way:
                exp_ref[:, cols] = part[k, z] + ring[n, way]
            else:
                total = exp_ref[:, cols] + ring[n, way]
                exp_ref[:, cols] = total
                pltpu.make_async_copy(exp_ref.at[:, cols], exp_hbm.at[:, cols], out_sem.at[0]).start()
                squares.append(squares_of(total))

    count_load.wait()
    loads[0].wait()
    live = lax.broadcasted_iota(jnp.int32, (HID, TOK), 1) < count_ref[0, 0]
    masked[...] = jnp.where(live, hidden[...].astype(jnp.float32), 0.0).astype(jnp.bfloat16)

    def exp_piece(k):
        loads[1 + k].wait()
        block = lax.dot_general(
            masked[...], cot[k], (((1,), (0,)), ((), ())), preferred_element_type=jnp.float32
        )
        part[k] = block.reshape(NZ, OWN, WIDE)

    core_copy = {}

    def att_group(g):
        if not ATT:
            return
        if g == 0:
            loads[1 + PIECES].wait()
            loads[2 + PIECES].wait()
        for i in (2 * g, 2 * g + 1):
            target = lax.rem(y + Y_ORDER[i], NY)
            columns = kv[:, pl.ds(pl.multiple_of(target * (KV2 // NY), KV2 // NY), KV2 // NY)]
            block = lax.dot_general(columns, xin[...], (((0,), (0,)), ((), ())), preferred_element_type=jnp.float32)
            grad[i] = block.reshape(NX, NC, ROWS, COLS)
        core_copy[g] = remote(
            grad.at[pl.ds(2 * g, 2), :, 1 - c], core_in.at[g], core_send.at[0], core_recv.at[g], at(z, y, x, 1 - c)
        )

    slots = ((0, 3, 1, 2), (0, 1, 3, 2))
    first_to = (x_rel[1], x_rel[3])
    second_to = (x_rel[3], x_rel[1])

    def att_first(g):
        if not ATT:
            return
        core_copy[g].wait_recv()
        for h in range(2):
            cols = pl.ds(h * HALF, HALF)
            for j in (2, 3):
                at_x = x_rel[slots[h][j]]
                for i in range(2):
                    send_a[g, h, j - 2, i] = grad[2 * g + i, at_x, c, :, cols] + core_in[g, i, at_x, :, cols]
            remote(
                send_a.at[g, h], recv_a.at[g, h], a_send.at[0], a_recv.at[g], at(z, y, first_to[h], c)
            )
        for h in range(2):
            cols = pl.ds(h * HALF, HALF)
            for j in (0, 1):
                at_x = x_rel[slots[h][j]]
                for i in range(2):
                    keep[g, h, j, i] = grad[2 * g + i, at_x, c, :, cols] + core_in[g, i, at_x, :, cols]

    def att_second(g):
        if not ATT:
            return
        arrived(recv_a.at[g], a_recv.at[g])
        for h in range(2):
            send_b[g, h] = keep[g, h, 1] + recv_a[g, h, 1]
            remote(
                send_b.at[g, h], recv_b.at[g, h], b_send.at[0], b_recv.at[g], at(z, y, second_to[h], c)
            )
            keep_b[g, h] = keep[g, h, 0] + recv_a[g, h, 0]

    def att_third(g):
        if not ATT:
            return
        arrived(recv_b.at[g], b_recv.at[g])
        for h in range(2):
            for i in range(2):
                y_out[2 * g + i, :, pl.ds(h * HALF, HALF)] = keep_b[g, h, i] + recv_b[g, h, i]
        for i in (2 * g, 2 * g + 1):
            d = Y_ORDER[i]
            if d:
                remote(
                    y_out.at[i], y_in.at[d - 1], y_send.at[0], y_recv.at[0], at(z, lax.rem(y + d, NY), x, c)
                )

    def att_last():
        if not ATT:
            return
        arrived(y_in, y_recv.at[0])
        total = y_out[Y_ORDER.index(0)]
        for d in Y_ORDER:
            if d:
                total = total + y_in[d - 1]
        att_ref[...] = total
        pltpu.make_async_copy(att_ref, att_hbm, out_sem.at[1]).start()
        squares.append(squares_of(total))

    work = {"second": att_second, "third": att_third, "last": lambda g: att_last()}

    pl.semaphore_wait(barrier, len(greeted))
    att_group(0)
    att_group(1)
    exp_piece(0)
    ring_start(0, 0)
    exp_piece(2)
    ring_start(1, 2)
    exp_piece(1)
    ring_start(0, 1)
    exp_piece(3)
    ring_start(1, 3)
    ring_start(0, 2)
    ring_start(1, 0)
    ring_start(0, 3)
    ring_start(1, 1)
    att_group(2)
    att_group(3)
    for g in range(GROUPS):
        att_first(g)
    for n in range(len(STEPS)):
        ring_step(n)
        for name, g in BETWEEN.get(n, ()):
            work[name](g)

    value = squares[0]
    for other in squares[1:]:
        value = value + other
    norm_c[...] = jnp.sum(value, axis=0, keepdims=True)

    def norm_copy(n, src, dst, device):
        return pltpu.make_async_remote_copy(
            src_ref=src, dst_ref=dst, send_sem=norm_send.at[n], recv_sem=norm_recv.at[n],
            device_id=device, device_id_type=MESH,
        )

    for d in (4, 3, 5, 2, 6, 1, 7):
        norm_copy(0, norm_c, norm_z.at[d * NC + c], at(lax.rem(z + d, NZ), y, x, 1)).start()

    @pl.when(c == 0)
    def _():
        norm_copy(0, norm_c, norm_z.at[0], at(z, y, x, 1)).start()

    for ref, sem in (
        (ring, ring_send), (core_in, core_send), (send_a, a_send), (send_b, b_send), (y_in, y_send), (exp_ref, out_sem)
    ):
        arrived(ref, sem.at[0])
    arrived(att_ref, out_sem.at[1])

    @pl.when(c == 0)
    def _():
        sent = norm_z.at[pl.ds(0, NZ)]
        pltpu.make_async_copy(sent, sent, norm_send.at[0]).wait()
        pltpu.make_async_copy(norm_p, norm_p, norm_recv.at[1]).wait()

    @pl.when(c == 1)
    def _():
        norm_z[1] = norm_c[...]
        others = norm_z.at[pl.ds(0, NZ * NC - 1)]
        pltpu.make_async_copy(others, others, norm_recv.at[0]).wait()
        norm_p[0] = jnp.sum(norm_z[...], axis=0)
        plane = [(dy, dx) for dy in range(NY) for dx in range(NX) if dy or dx]
        plane.sort(key=lambda e: -min(e[0], NY - e[0]) - min(e[1], NX - e[1]))
        for core in range(NC):
            for dy, dx in plane if core else plane + [(0, 0)]:
                device = at(z, lax.rem(y + dy, NY), lax.rem(x + dx, NX), core)
                norm_copy(1, norm_p.at[0], norm_p.at[dy * NX + dx], device).start()
        sent = norm_z.at[pl.ds(0, NZ - 1)]
        pltpu.make_async_copy(sent, sent, norm_send.at[0]).wait()
        others = norm_p.at[pl.ds(1, NX * NY - 1)]
        pltpu.make_async_copy(others, others, norm_recv.at[1]).wait()
        for sent in (norm_p, others):
            pltpu.make_async_copy(sent, sent, norm_send.at[1]).wait()

    norm_ref[...] = jnp.sum(norm_p[...], axis=0)


def grads(hidden, cot, kv, xin, counts):
    f32, bf16 = jnp.float32, jnp.bfloat16
    dma = pltpu.SemaphoreType.DMA
    hbm = pl.BlockSpec(memory_space=pltpu.HBM)
    vmem = pl.BlockSpec(memory_space=pltpu.VMEM)
    return pl.pallas_call(
        grads_kernel,
        out_shape=tuple(jax.ShapeDtypeStruct(shape, f32) for shape in ((OWN, DW), (ROWS, COLS), (1, 128))),
        in_specs=[hbm] * 5,
        out_specs=(hbm, hbm, vmem),
        scratch_shapes=[
            pltpu.VMEM((OWN, DW), f32),
            pltpu.VMEM((ROWS, COLS), f32),
            pltpu.SMEM((1, 1), jnp.int32),
            pltpu.VMEM((HID, TOK), bf16),
            pltpu.VMEM((PIECES, TOK, WIDE), bf16),
            pltpu.VMEM((TOK, KV2), bf16),
            pltpu.VMEM((TOK, COLS), bf16),
            pltpu.VMEM((HID, TOK), bf16),
            pltpu.VMEM((PIECES, NZ, OWN, WIDE), f32),
            pltpu.VMEM((len(STEPS), 2, OWN, WIDE), f32),
            pltpu.VMEM((NY, NX, NC, ROWS, COLS), f32),
            pltpu.VMEM((GROUPS, 2, NX, ROWS, COLS), f32),
            pltpu.VMEM((GROUPS, 2, 2, 2, ROWS, HALF), f32),
            pltpu.VMEM((GROUPS, 2, 2, 2, ROWS, HALF), f32),
            pltpu.VMEM((GROUPS, 2, 2, 2, ROWS, HALF), f32),
            pltpu.VMEM((GROUPS, 2, 2, ROWS, HALF), f32),
            pltpu.VMEM((GROUPS, 2, 2, ROWS, HALF), f32),
            pltpu.VMEM((GROUPS, 2, 2, ROWS, HALF), f32),
            pltpu.VMEM((NY, ROWS, COLS), f32),
            pltpu.VMEM((NY - 1, ROWS, COLS), f32),
            pltpu.VMEM((1, 128), f32),
            pltpu.VMEM((NZ * NC, 1, 128), f32),
            pltpu.VMEM((NX * NY, 1, 128), f32),
            dma((4 + PIECES,)),
            dma((1,)),
            dma((len(STEPS),)),
            dma((1,)),
            dma((GROUPS,)),
            dma((1,)),
            dma((GROUPS,)),
            dma((1,)),
            dma((GROUPS,)),
            dma((1,)),
            dma((1,)),
            dma((2,)),
            dma((2,)),
            dma((2,)),
        ],
        compiler_params=pltpu.CompilerParams(
            collective_id=0, has_side_effects=True, vmem_limit_bytes=55091 * 1024
        ),
        name="grads",
    )(hidden, cot, kv, xin, counts)


BLOCKS = 4


def update_kernel(norm_hbm, *refs):
    att_in, exp_in, att_out, exp_out = refs[0:4], refs[4:8], refs[8:11], refs[11:14]
    norm, att, exp, new_att, new_exp, load_sem, store_sem = refs[14:]
    wide = DW // BLOCKS
    cols = [pl.ds(n * wide, wide) for n in range(BLOCKS)]
    pltpu.make_async_copy(norm_hbm, norm, load_sem.at[0]).start()
    for i, a in enumerate(att_in):
        pltpu.make_async_copy(a, att.at[i], load_sem.at[1]).start()
    for n in range(BLOCKS):
        for i, a in enumerate(exp_in):
            pltpu.make_async_copy(a.at[:, cols[n]], exp.at[i, :, cols[n]], load_sem.at[2 + n]).start()

    def arrived(ref, sem):
        pltpu.make_async_copy(ref, ref, sem).wait()

    def block(values, keep, sources, targets, sem):
        new = adam_update(*values, clip)
        for i in range(3):
            keep(i, new[i])
            pltpu.make_async_copy(sources[i], targets[i], sem).start()

    arrived(norm, load_sem.at[0])
    arrived(att, load_sem.at[1])
    entries = float(KV2 * D + NY * NX * NC // GROUP * FF * DW)
    square_sum = jnp.sum(norm[...], axis=1, keepdims=True)
    clip = jnp.minimum(1.0, jnp.sqrt(jnp.full_like(square_sum, entries)) / (jnp.sqrt(square_sum) + 1e-06))

    def keep_att(i, value):
        new_att[i] = value

    block([att[i] for i in range(4)], keep_att, [new_att.at[i] for i in range(3)], att_out, store_sem.at[0])
    for n in range(BLOCKS):
        arrived(exp.at[:, :, cols[n]], load_sem.at[2 + n])

        def keep_exp(i, value):
            new_exp[i, :, cols[n]] = value

        block(
            [exp[i, :, cols[n]] for i in range(4)],
            keep_exp,
            [new_exp.at[i, :, cols[n]] for i in range(3)],
            [ref.at[:, cols[n]] for ref in exp_out],
            store_sem.at[1],
        )
    arrived(new_att, store_sem.at[0])
    arrived(new_exp, store_sem.at[1])


def update(norm, att, exp):
    f32 = jnp.float32
    hbm = pl.BlockSpec(memory_space=pltpu.HBM)
    return pl.pallas_call(
        update_kernel,
        out_shape=tuple(jax.ShapeDtypeStruct(a.shape, f32) for a in (*att[:3], *exp[:3])),
        in_specs=[hbm] * 9,
        out_specs=(hbm,) * 6,
        scratch_shapes=[
            pltpu.VMEM((1, 128), f32),
            pltpu.VMEM((4, ROWS, COLS), f32),
            pltpu.VMEM((4, OWN, DW), f32),
            pltpu.VMEM((3, ROWS, COLS), f32),
            pltpu.VMEM((3, OWN, DW), f32),
            pltpu.SemaphoreType.DMA((2 + BLOCKS,)),
            pltpu.SemaphoreType.DMA((2,)),
        ],
        compiler_params=pltpu.CompilerParams(vmem_limit_bytes=55091 * 1024),
        name="update",
    )(norm, *att, *exp)


def on_device(
    att_input,
    kv_cotangent,
    expert_hidden,
    expert_cotangent,
    token_counts,
    att_param,
    att_moment,
    att_second,
    exp_param,
    exp_moment,
    exp_second,
):
    exp_grad, att_grad, norm = grads(expert_hidden.T, expert_cotangent, kv_cotangent, att_input, token_counts)
    return update(
        norm,
        (att_param, att_moment, att_second, att_grad),
        (exp_param, exp_moment, exp_second, exp_grad),
    )


def solution(mesh):
    in_specs = (
        P("dp", "expert"),
        P("dp", None),
        P("expert", "dp"),
        P("expert", "dp"),
        P("dp", "expert"),
        P("dp", "expert"),
        P("dp", "expert"),
        P("dp", "expert"),
        P(("dp", "expert"), None),
        P(("dp", "expert"), None),
        P(("dp", "expert"), None),
    )
    out_specs = (
        P("dp", "expert"),
        P("dp", "expert"),
        P("dp", "expert"),
        P(("dp", "expert"), None),
        P(("dp", "expert"), None),
        P(("dp", "expert"), None),
    )
    return jax.shard_map(
        on_device, mesh=mesh, in_specs=in_specs, out_specs=out_specs, check_vma=False
    )
```

```python
import functools

import jax
import jax.numpy as jnp
from jax import lax
from jax.experimental import pallas as pl
from jax.experimental.pallas import tpu as pltpu
from jax.sharding import PartitionSpec as P

D = 4096
KV2 = 1024
FF = 1536
DW = 2048
GROUP = 8

beta_one = 0.9
beta_two = 0.95
learn_rate = 0.01
decay_rate = 0.1
epsilon = 1e-08
step_number = 5

NX, NY, NZ, NC = 4, 8, 8, 2
TOK = 384
HID = 192
OWN = HID // NZ
HALVES = 2
SPLIT = 2
PIECES = HALVES * SPLIT
WIDE = DW // PIECES
DEPTH = NZ // 2
STEPS = [
    (DEPTH - (unit + 1) // 2, unit % 2 * SPLIT + p, (1 - unit % 2) * SPLIT + p)
    for unit in range(2 * DEPTH - 1)
    for p in range(SPLIT)
]
SLOTS = {(way, step[1 + way], step[0]): (n, way) for n, step in enumerate(STEPS) for way in range(2)}
COLS = 512
MAIN = COLS - 128
ROWS = 16
HALF = ROWS // 2
GROUPS = 4
Y_ORDER = (4, 3, 5, 2, 6, 1, 7, 0)
MESH = pl.DeviceIdType.MESH
RING, ATT, NORM = True, True, True
BETWEEN = {
    1: (('second', 0),),
    2: (('second', 1),),
    3: (('second', 2),),
    5: (('second', 3), ('third', 0)),
    6: (('third', 1),),
    7: (('third', 2), ('cross', 0)),
    8: (('third', 3),),
    11: (('last', 0),),
}


def adam_update(param, moment, second, grad, clip):
    scaled = clip * grad
    new_moment = beta_one * moment + (1.0 - beta_one) * scaled
    new_second = beta_two * second + (1.0 - beta_two) * scaled * scaled
    fix_one = 1.0 - beta_one**step_number
    fix_two = 1.0 - beta_two**step_number
    update = new_moment / fix_one / (jnp.sqrt(new_second / fix_two) + epsilon)
    new_param = param - learn_rate * (update + decay_rate * param)
    return (new_param, new_moment, new_second)


def grads_kernel(
    hidden_hbm, cot_hbm, kv_hbm, x_hbm, count_hbm,
    exp_hbm, att_hbm, norm_ref,
    exp_ref, att_ref, count_ref, hidden, cot, kv, xin, masked, part, ring, grad, core_in, keep, send_a, recv_a, keep_b, send_b, recv_b, y_out, y_in,
    side, side_in, cross, cross_in,
    norm_c, norm_z, norm_p,
    load_sem, ring_send, ring_recv, core_send, core_recv, a_send, a_recv, b_send, b_recv, y_send, y_recv, side_send, side_recv, cross_send, cross_recv, norm_send, norm_recv, out_sem,
):
    dp = lax.axis_index("dp")
    z = lax.axis_index("expert")
    c = lax.rem(dp, NC)
    x = lax.rem(dp // NC, NX)
    y = dp // (NC * NX)

    def at(zz, yy, xx, cc):
        return ((yy * NX + xx) * NC + cc, zz)

    x_rel = (x, x + 1 - 2 * lax.rem(x, 2), lax.rem(x + 2, NX), NX - 1 - x)

    barrier = pltpu.get_barrier_semaphore()
    greeted = [at(lax.rem(z + 1, NZ), y, x, c), at(lax.rem(z + NZ - 1, NZ), y, x, c), at(z, y, x, 1 - c)]
    greeted += [at(z, y, x_rel[r], c) for r in range(1, NX)]
    greeted += [at(z, lax.rem(y + d, NY), x, c) for d in range(1, NY)]
    for device in greeted:
        pl.semaphore_signal(barrier, inc=1, device_id=device, device_id_type=MESH)

    loads = [pltpu.make_async_copy(hidden_hbm, hidden, load_sem.at[0])]
    for k in range(PIECES):
        loads.append(pltpu.make_async_copy(cot_hbm.at[:, pl.ds(k * WIDE, WIDE)], cot.at[k], load_sem.at[1 + k]))
    loads.append(pltpu.make_async_copy(x_hbm, xin, load_sem.at[1 + PIECES]))
    loads.append(pltpu.make_async_copy(kv_hbm, kv, load_sem.at[2 + PIECES]))
    count_load = pltpu.make_async_copy(count_hbm, count_ref, load_sem.at[3 + PIECES])
    count_load.start()
    for n in (1 + PIECES, 2 + PIECES, *range(1 + PIECES)):
        loads[n].start()

    def squares_of(value):
        rows, width = value.shape
        value = value * value
        total = value[0:8, 0:128]
        for i in range(0, rows, 8):
            for j in range(0, width, 128):
                if i or j:
                    total = total + value[i : i + 8, j : j + 128]
        return total

    def arrived(ref, sem):
        pltpu.make_async_copy(ref, ref, sem).wait()

    def remote(src, dst, send_sem, recv_sem, device):
        copy = pltpu.make_async_remote_copy(
            src_ref=src, dst_ref=dst, send_sem=send_sem, recv_sem=recv_sem, device_id=device, device_id_type=MESH
        )
        copy.start()
        return copy

    towards = (at(lax.rem(z + NZ - 1, NZ), y, x, c), at(lax.rem(z + 1, NZ), y, x, c))

    def shard(way, hops):
        return lax.rem(z + NZ - hops, NZ) if way == 0 else lax.rem(z + hops, NZ)

    def ring_send_step(way, k, hops, src):
        if not RING:
            return
        n, _ = SLOTS[way, k, hops]
        remote(src, ring.at[n, way], ring_send.at[0], ring_recv.at[n], towards[way])

    def ring_start(way, k):
        if not RING:
            return
        hops = DEPTH if k // SPLIT == way else DEPTH - 1
        ring_send_step(way, k, hops, part.at[k, shard(way, hops)])

    squares = []

    def ring_step(n):
        hops, down, up = STEPS[n]
        left = hops - 1
        arrived(ring.at[n], ring_recv.at[n])
        for way, k in enumerate((down, up)):
            if left:
                ring[n, way] = ring[n, way] + part[k, shard(way, left)]
                ring_send_step(way, k, left, ring.at[n, way])
                continue
            cols = pl.ds(k * WIDE, WIDE)
            if k // SPLIT != way:
                exp_ref[:, cols] = part[k, z] + ring[n, way]
            else:
                total = exp_ref[:, cols] + ring[n, way]
                exp_ref[:, cols] = total
                pltpu.make_async_copy(exp_ref.at[:, cols], exp_hbm.at[:, cols], out_sem.at[0]).start()
                squares.append(squares_of(total))

    count_load.wait()
    loads[0].wait()
    live = lax.broadcasted_iota(jnp.int32, (HID, TOK), 1) < count_ref[0, 0]
    masked[...] = jnp.where(live, hidden[...].astype(jnp.float32), 0.0).astype(jnp.bfloat16)

    def exp_piece(k):
        loads[1 + k].wait()
        block = lax.dot_general(
            masked[...], cot[k], (((1,), (0,)), ((), ())), preferred_element_type=jnp.float32
        )
        part[k] = block.reshape(NZ, OWN, WIDE)

    core_copy = {}

    def att_group(g):
        if not ATT:
            return
        if g == 0:
            loads[1 + PIECES].wait()
            loads[2 + PIECES].wait()
        for i in (2 * g, 2 * g + 1):
            target = lax.rem(y + Y_ORDER[i], NY)
            columns = kv[:, pl.ds(pl.multiple_of(target * (KV2 // NY), KV2 // NY), KV2 // NY)]
            block = lax.dot_general(columns, xin[...], (((0,), (0,)), ((), ())), preferred_element_type=jnp.float32)
            grad[i] = block.reshape(NX, NC, ROWS, COLS)
        core_copy[g] = remote(
            grad.at[pl.ds(2 * g, 2), :, 1 - c], core_in.at[g], core_send.at[0], core_recv.at[g], at(z, y, x, 1 - c)
        )

    slots = ((0, 3, 1, 2), (0, 1, 3, 2))
    first_to = (x_rel[1], x_rel[3])
    second_to = (x_rel[3], x_rel[1])

    def att_first(g):
        arrived(core_in.at[g], core_recv.at[g])
        for h in range(2):
            rows, cols = pl.ds(h * HALF, HALF), pl.ds(0, MAIN)
            for j in (2, 3):
                at_x = x_rel[slots[h][j]]
                for i in range(2):
                    send_a[g, h, j - 2, i] = grad[2 * g + i, at_x, c, rows, cols] + core_in[g, i, at_x, rows, cols]
            remote(send_a.at[g, h], recv_a.at[g, h], a_send.at[0], a_recv.at[g], at(z, y, first_to[h], c))
        for i in (2 * g, 2 * g + 1):
            d, cols = Y_ORDER[i], pl.ds(MAIN, COLS - MAIN)
            for at_x in range(NX):
                side[d, at_x] = grad[i, at_x, c, :, cols] + core_in[g, i - 2 * g, at_x, :, cols]
            if d:
                remote(side.at[d], side_in.at[d - 1], side_send.at[0], side_recv.at[0], at(z, lax.rem(y + d, NY), x, c))
        for h in range(2):
            rows, cols = pl.ds(h * HALF, HALF), pl.ds(0, MAIN)
            for j in (0, 1):
                at_x = x_rel[slots[h][j]]
                for i in range(2):
                    keep[g, h, j, i] = grad[2 * g + i, at_x, c, rows, cols] + core_in[g, i, at_x, rows, cols]

    def att_second(g):
        arrived(recv_a.at[g], a_recv.at[g])
        for h in range(2):
            send_b[g, h] = keep[g, h, 1] + recv_a[g, h, 1]
            remote(send_b.at[g, h], recv_b.at[g, h], b_send.at[0], b_recv.at[g], at(z, y, second_to[h], c))
        for h in range(2):
            keep_b[g, h] = keep[g, h, 0] + recv_a[g, h, 0]

    def att_third(g):
        arrived(recv_b.at[g], b_recv.at[g])
        for h in range(2):
            for i in range(2):
                y_out[2 * g + i, pl.ds(h * HALF, HALF)] = keep_b[g, h, i] + recv_b[g, h, i]
        for i in (2 * g, 2 * g + 1):
            d = Y_ORDER[i]
            if d:
                remote(y_out.at[i], y_in.at[d - 1], y_send.at[0], y_recv.at[0], at(z, lax.rem(y + d, NY), x, c))

    def att_cross(g):
        arrived(side_in, side_recv.at[0])
        total = side[0]
        for d in range(1, NY):
            total = total + side_in[d - 1]
        cross[...] = total
        for r in (2, 1, 3):
            remote(cross.at[x_rel[r]], cross_in.at[r - 1], cross_send.at[0], cross_recv.at[0], at(z, y, x_rel[r], c))

    def att_last(g):
        arrived(cross_in, cross_recv.at[0])
        total = cross[x]
        for r in range(1, NX):
            total = total + cross_in[r - 1]
        att_ref[:, pl.ds(MAIN, COLS - MAIN)] = total
        squares.append(squares_of(total))
        arrived(y_in, y_recv.at[0])
        total = y_out[Y_ORDER.index(0)]
        for d in range(1, NY):
            total = total + y_in[d - 1]
        att_ref[:, pl.ds(0, MAIN)] = total
        squares.append(squares_of(total))
        pltpu.make_async_copy(att_ref, att_hbm, out_sem.at[1]).start()

    work = {"second": att_second, "third": att_third, "cross": att_cross, "last": att_last}

    exp_piece(0)
    pl.semaphore_wait(barrier, len(greeted))
    ring_start(0, 0)
    exp_piece(2)
    ring_start(1, 2)
    exp_piece(1)
    ring_start(0, 1)
    exp_piece(3)
    ring_start(1, 3)
    ring_start(0, 2)
    ring_start(1, 0)
    ring_start(0, 3)
    ring_start(1, 1)
    att_group(0)
    att_group(1)
    att_group(2)
    att_group(3)
    for g in range(GROUPS):
        att_first(g)
    for n in range(len(STEPS)):
        ring_step(n)
        for name, g in BETWEEN.get(n, ()):
            work[name](g)

    value = squares[0]
    for other in squares[1:]:
        value = value + other
    norm_c[...] = jnp.sum(value, axis=0, keepdims=True)

    def norm_copy(n, src, dst, device):
        return pltpu.make_async_remote_copy(
            src_ref=src, dst_ref=dst, send_sem=norm_send.at[n], recv_sem=norm_recv.at[n],
            device_id=device, device_id_type=MESH,
        )

    for d in (4, 3, 5, 2, 6, 1, 7):
        norm_copy(0, norm_c, norm_z.at[d * NC + c], at(lax.rem(z + d, NZ), y, x, 1)).start()

    @pl.when(c == 0)
    def _():
        norm_copy(0, norm_c, norm_z.at[0], at(z, y, x, 1)).start()

    for ref, sem in (
        (ring, ring_send), (core_in, core_send), (send_a, a_send), (send_b, b_send), (y_in, y_send), (exp_ref, out_sem),
        (side_in, side_send), (cross_in, cross_send),
    ):
        arrived(ref, sem.at[0])
    arrived(att_ref, out_sem.at[1])

    @pl.when(c == 0)
    def _():
        sent = norm_z.at[pl.ds(0, NZ)]
        pltpu.make_async_copy(sent, sent, norm_send.at[0]).wait()
        pltpu.make_async_copy(norm_p, norm_p, norm_recv.at[1]).wait()

    @pl.when(c == 1)
    def _():
        norm_z[1] = norm_c[...]
        others = norm_z.at[pl.ds(0, NZ * NC - 1)]
        pltpu.make_async_copy(others, others, norm_recv.at[0]).wait()
        norm_p[0] = jnp.sum(norm_z[...], axis=0)
        plane = [(dy, dx) for dy in range(NY) for dx in range(NX) if dy or dx]
        plane.sort(key=lambda e: -min(e[0], NY - e[0]) - min(e[1], NX - e[1]))
        for core in range(NC):
            for dy, dx in plane if core else plane + [(0, 0)]:
                device = at(z, lax.rem(y + dy, NY), lax.rem(x + dx, NX), core)
                norm_copy(1, norm_p.at[0], norm_p.at[dy * NX + dx], device).start()
        sent = norm_z.at[pl.ds(0, NZ - 1)]
        pltpu.make_async_copy(sent, sent, norm_send.at[0]).wait()
        others = norm_p.at[pl.ds(1, NX * NY - 1)]
        pltpu.make_async_copy(others, others, norm_recv.at[1]).wait()
        for sent in (norm_p, others):
            pltpu.make_async_copy(sent, sent, norm_send.at[1]).wait()

    norm_ref[...] = jnp.sum(norm_p[...], axis=0)


def grads(hidden, cot, kv, xin, counts):
    f32, bf16 = jnp.float32, jnp.bfloat16
    dma = pltpu.SemaphoreType.DMA
    hbm = pl.BlockSpec(memory_space=pltpu.HBM)
    vmem = pl.BlockSpec(memory_space=pltpu.VMEM)
    return pl.pallas_call(
        grads_kernel,
        out_shape=tuple(jax.ShapeDtypeStruct(shape, f32) for shape in ((OWN, DW), (ROWS, COLS), (1, 128))),
        in_specs=[hbm] * 5,
        out_specs=(hbm, hbm, vmem),
        scratch_shapes=[
            pltpu.VMEM((OWN, DW), f32),
            pltpu.VMEM((ROWS, COLS), f32),
            pltpu.SMEM((1, 1), jnp.int32),
            pltpu.VMEM((HID, TOK), bf16),
            pltpu.VMEM((PIECES, TOK, WIDE), bf16),
            pltpu.VMEM((TOK, KV2), bf16),
            pltpu.VMEM((TOK, COLS), bf16),
            pltpu.VMEM((HID, TOK), bf16),
            pltpu.VMEM((PIECES, NZ, OWN, WIDE), f32),
            pltpu.VMEM((len(STEPS), 2, OWN, WIDE), f32),
            pltpu.VMEM((NY, NX, NC, ROWS, COLS), f32),
            pltpu.VMEM((GROUPS, 2, NX, ROWS, COLS), f32),
            pltpu.VMEM((GROUPS, 2, 2, 2, HALF, MAIN), f32),
            pltpu.VMEM((GROUPS, 2, 2, 2, HALF, MAIN), f32),
            pltpu.VMEM((GROUPS, 2, 2, 2, HALF, MAIN), f32),
            pltpu.VMEM((GROUPS, 2, 2, HALF, MAIN), f32),
            pltpu.VMEM((GROUPS, 2, 2, HALF, MAIN), f32),
            pltpu.VMEM((GROUPS, 2, 2, HALF, MAIN), f32),
            pltpu.VMEM((NY, ROWS, MAIN), f32),
            pltpu.VMEM((NY - 1, ROWS, MAIN), f32),
            pltpu.VMEM((NY, NX, ROWS, COLS - MAIN), f32),
            pltpu.VMEM((NY - 1, NX, ROWS, COLS - MAIN), f32),
            pltpu.VMEM((NX, ROWS, COLS - MAIN), f32),
            pltpu.VMEM((NX - 1, ROWS, COLS - MAIN), f32),
            pltpu.VMEM((1, 128), f32),
            pltpu.VMEM((NZ * NC, 1, 128), f32),
            pltpu.VMEM((NX * NY, 1, 128), f32),
            dma((4 + PIECES,)),
            dma((1,)),
            dma((len(STEPS),)),
            dma((1,)),
            dma((GROUPS,)),
            dma((1,)),
            dma((GROUPS,)),
            dma((1,)),
            dma((GROUPS,)),
            dma((1,)),
            dma((1,)),
            dma((1,)),
            dma((1,)),
            dma((1,)),
            dma((1,)),
            dma((2,)),
            dma((2,)),
            dma((2,)),
        ],
        compiler_params=pltpu.CompilerParams(
            collective_id=0, has_side_effects=True, vmem_limit_bytes=55091 * 1024
        ),
        name="grads",
    )(hidden, cot, kv, xin, counts)


BLOCKS = 4


def update_kernel(norm_hbm, *refs):
    att_in, exp_in, att_out, exp_out = refs[0:4], refs[4:8], refs[8:11], refs[11:14]
    norm, att, exp, new_att, new_exp, load_sem, store_sem = refs[14:]
    wide = DW // BLOCKS
    cols = [pl.ds(n * wide, wide) for n in range(BLOCKS)]
    pltpu.make_async_copy(norm_hbm, norm, load_sem.at[0]).start()
    for i, a in enumerate(att_in):
        pltpu.make_async_copy(a, att.at[i], load_sem.at[1]).start()
    for n in range(BLOCKS):
        for i, a in enumerate(exp_in):
            pltpu.make_async_copy(a.at[:, cols[n]], exp.at[i, :, cols[n]], load_sem.at[2 + n]).start()

    def arrived(ref, sem):
        pltpu.make_async_copy(ref, ref, sem).wait()

    def block(values, keep, sources, targets, sem):
        new = adam_update(*values, clip)
        for i in range(3):
            keep(i, new[i])
            pltpu.make_async_copy(sources[i], targets[i], sem).start()

    arrived(norm, load_sem.at[0])
    arrived(att, load_sem.at[1])
    entries = float(KV2 * D + NY * NX * NC // GROUP * FF * DW)
    square_sum = jnp.sum(norm[...], axis=1, keepdims=True)
    clip = jnp.minimum(1.0, jnp.sqrt(jnp.full_like(square_sum, entries)) / (jnp.sqrt(square_sum) + 1e-06))

    def keep_att(i, value):
        new_att[i] = value

    block([att[i] for i in range(4)], keep_att, [new_att.at[i] for i in range(3)], att_out, store_sem.at[0])
    for n in range(BLOCKS):
        arrived(exp.at[:, :, cols[n]], load_sem.at[2 + n])

        def keep_exp(i, value):
            new_exp[i, :, cols[n]] = value

        block(
            [exp[i, :, cols[n]] for i in range(4)],
            keep_exp,
            [new_exp.at[i, :, cols[n]] for i in range(3)],
            [ref.at[:, cols[n]] for ref in exp_out],
            store_sem.at[1],
        )
    arrived(new_att, store_sem.at[0])
    arrived(new_exp, store_sem.at[1])


def update(norm, att, exp):
    f32 = jnp.float32
    hbm = pl.BlockSpec(memory_space=pltpu.HBM)
    return pl.pallas_call(
        update_kernel,
        out_shape=tuple(jax.ShapeDtypeStruct(a.shape, f32) for a in (*att[:3], *exp[:3])),
        in_specs=[hbm] * 9,
        out_specs=(hbm,) * 6,
        scratch_shapes=[
            pltpu.VMEM((1, 128), f32),
            pltpu.VMEM((4, ROWS, COLS), f32),
            pltpu.VMEM((4, OWN, DW), f32),
            pltpu.VMEM((3, ROWS, COLS), f32),
            pltpu.VMEM((3, OWN, DW), f32),
            pltpu.SemaphoreType.DMA((2 + BLOCKS,)),
            pltpu.SemaphoreType.DMA((2,)),
        ],
        compiler_params=pltpu.CompilerParams(vmem_limit_bytes=55091 * 1024),
        name="update",
    )(norm, *att, *exp)


def on_device(
    att_input,
    kv_cotangent,
    expert_hidden,
    expert_cotangent,
    token_counts,
    att_param,
    att_moment,
    att_second,
    exp_param,
    exp_moment,
    exp_second,
):
    exp_grad, att_grad, norm = grads(expert_hidden.T, expert_cotangent, kv_cotangent, att_input, token_counts)
    return update(
        norm,
        (att_param, att_moment, att_second, att_grad),
        (exp_param, exp_moment, exp_second, exp_grad),
    )


def solution(mesh):
    in_specs = (
        P("dp", "expert"),
        P("dp", None),
        P("expert", "dp"),
        P("expert", "dp"),
        P("dp", "expert"),
        P("dp", "expert"),
        P("dp", "expert"),
        P("dp", "expert"),
        P(("dp", "expert"), None),
        P(("dp", "expert"), None),
        P(("dp", "expert"), None),
    )
    out_specs = (
        P("dp", "expert"),
        P("dp", "expert"),
        P("dp", "expert"),
        P(("dp", "expert"), None),
        P(("dp", "expert"), None),
        P(("dp", "expert"), None),
    )
    return jax.shard_map(
        on_device, mesh=mesh, in_specs=in_specs, out_specs=out_specs, check_vma=False
    )
```

```python
import functools

import jax
import jax.numpy as jnp
from jax import lax
from jax.experimental import pallas as pl
from jax.experimental.pallas import tpu as pltpu
from jax.sharding import PartitionSpec as P

D = 4096
KV2 = 1024
FF = 1536
DW = 2048
GROUP = 8

beta_one = 0.9
beta_two = 0.95
learn_rate = 0.01
decay_rate = 0.1
epsilon = 1e-08
step_number = 5

NX, NY, NZ, NC = 4, 8, 8, 2
TOK = 384
HID = 192
OWN = HID // NZ
HALVES = 2
SPLIT = 2
PIECES = HALVES * SPLIT
WIDE = DW // PIECES
DEPTH = NZ // 2
STEPS = [
    (DEPTH - (unit + 1) // 2, unit % 2 * SPLIT + p, (1 - unit % 2) * SPLIT + p)
    for unit in range(2 * DEPTH - 1)
    for p in range(SPLIT)
]
SLOTS = {(way, step[1 + way], step[0]): (n, way) for n, step in enumerate(STEPS) for way in range(2)}
COLS = 512
MAIN = COLS - 128
ROWS = 16
HALF = ROWS // 2
GROUPS = 4
Y_ORDER = (4, 3, 5, 2, 6, 1, 7, 0)
MESH = pl.DeviceIdType.MESH
RING, ATT, NORM = True, True, True
BETWEEN = {
    1: (('second', 0),),
    2: (('second', 1),),
    3: (('second', 2),),
    5: (('second', 3), ('third', 0)),
    6: (('third', 1),),
    7: (('third', 2), ('cross', 0)),
    8: (('third', 3),),
    11: (('last', 0),),
}


def adam_update(param, moment, second, grad, clip):
    scaled = clip * grad
    new_moment = beta_one * moment + (1.0 - beta_one) * scaled
    new_second = beta_two * second + (1.0 - beta_two) * scaled * scaled
    fix_one = 1.0 - beta_one**step_number
    fix_two = 1.0 - beta_two**step_number
    update = new_moment / fix_one / (jnp.sqrt(new_second / fix_two) + epsilon)
    new_param = param - learn_rate * (update + decay_rate * param)
    return (new_param, new_moment, new_second)


def grads_kernel(
    hidden_hbm, cot_hbm, kv_hbm, x_hbm, count_hbm,
    exp_hbm, att_hbm, norm_ref,
    exp_ref, att_ref, count_ref, hidden, cot, kv, xin, masked, part, ring, grad, core_in, keep, send_a, recv_a, keep_b, send_b, recv_b, y_out, y_in,
    side, side_in, cross, cross_in,
    norm_c, norm_z, norm_p,
    load_sem, ring_send, ring_recv, core_send, core_recv, a_send, a_recv, b_send, b_recv, y_send, y_recv, side_send, side_recv, cross_send, cross_recv, norm_send, norm_recv, out_sem,
):
    dp = lax.axis_index("dp")
    z = lax.axis_index("expert")
    c = lax.rem(dp, NC)
    x = lax.rem(dp // NC, NX)
    y = dp // (NC * NX)

    def at(zz, yy, xx, cc):
        return ((yy * NX + xx) * NC + cc, zz)

    x_rel = (x, x + 1 - 2 * lax.rem(x, 2), lax.rem(x + 2, NX), NX - 1 - x)

    barrier = pltpu.get_barrier_semaphore()
    greeted = [at(lax.rem(z + 1, NZ), y, x, c), at(lax.rem(z + NZ - 1, NZ), y, x, c), at(z, y, x, 1 - c)]
    greeted += [at(z, y, x_rel[r], c) for r in range(1, NX)]
    greeted += [at(z, lax.rem(y + d, NY), x, c) for d in range(1, NY)]
    for device in greeted:
        pl.semaphore_signal(barrier, inc=1, device_id=device, device_id_type=MESH)

    loads = [pltpu.make_async_copy(hidden_hbm, hidden, load_sem.at[0])]
    for k in range(PIECES):
        loads.append(pltpu.make_async_copy(cot_hbm.at[:, pl.ds(k * WIDE, WIDE)], cot.at[k], load_sem.at[1 + k]))
    loads.append(pltpu.make_async_copy(x_hbm, xin, load_sem.at[1 + PIECES]))
    loads.append(pltpu.make_async_copy(kv_hbm, kv, load_sem.at[2 + PIECES]))
    count_load = pltpu.make_async_copy(count_hbm, count_ref, load_sem.at[3 + PIECES])
    count_load.start()
    for n in (0, 1, 1 + SPLIT, 2, 2 + SPLIT, 1 + PIECES, 2 + PIECES):
        loads[n].start()

    def squares_of(value):
        rows, width = value.shape
        value = value * value
        total = value[0:8, 0:128]
        for i in range(0, rows, 8):
            for j in range(0, width, 128):
                if i or j:
                    total = total + value[i : i + 8, j : j + 128]
        return total

    def arrived(ref, sem):
        pltpu.make_async_copy(ref, ref, sem).wait()

    def remote(src, dst, send_sem, recv_sem, device):
        copy = pltpu.make_async_remote_copy(
            src_ref=src, dst_ref=dst, send_sem=send_sem, recv_sem=recv_sem, device_id=device, device_id_type=MESH
        )
        copy.start()
        return copy

    towards = (at(lax.rem(z + NZ - 1, NZ), y, x, c), at(lax.rem(z + 1, NZ), y, x, c))

    def shard(way, hops):
        return lax.rem(z + NZ - hops, NZ) if way == 0 else lax.rem(z + hops, NZ)

    def ring_send_step(way, k, hops, src):
        if not RING:
            return
        n, _ = SLOTS[way, k, hops]
        remote(src, ring.at[n, way], ring_send.at[0], ring_recv.at[n], towards[way])

    def ring_start(way, k):
        if not RING:
            return
        hops = DEPTH if k // SPLIT == way else DEPTH - 1
        ring_send_step(way, k, hops, part.at[k, shard(way, hops)])

    squares = []

    def ring_step(n):
        hops, down, up = STEPS[n]
        left = hops - 1
        arrived(ring.at[n], ring_recv.at[n])
        for way, k in enumerate((down, up)):
            if left:
                ring[n, way] = ring[n, way] + part[k, shard(way, left)]
                ring_send_step(way, k, left, ring.at[n, way])
                continue
            cols = pl.ds(k * WIDE, WIDE)
            if k // SPLIT != way:
                exp_ref[:, cols] = part[k, z] + ring[n, way]
            else:
                total = exp_ref[:, cols] + ring[n, way]
                exp_ref[:, cols] = total
                pltpu.make_async_copy(exp_ref.at[:, cols], exp_hbm.at[:, cols], out_sem.at[0]).start()
                squares.append(squares_of(total))

    count_load.wait()
    loads[0].wait()
    live = lax.broadcasted_iota(jnp.int32, (HID, TOK), 1) < count_ref[0, 0]
    masked[...] = jnp.where(live, hidden[...].astype(jnp.float32), 0.0).astype(jnp.bfloat16)

    def exp_piece(k):
        loads[1 + k].wait()
        block = lax.dot_general(
            masked[...], cot[k], (((1,), (0,)), ((), ())), preferred_element_type=jnp.float32
        )
        part[k] = block.reshape(NZ, OWN, WIDE)

    core_copy = {}

    def att_group(g):
        if not ATT:
            return
        if g == 0:
            loads[1 + PIECES].wait()
            loads[2 + PIECES].wait()
        for i in (2 * g, 2 * g + 1):
            target = lax.rem(y + Y_ORDER[i], NY)
            columns = kv[:, pl.ds(pl.multiple_of(target * (KV2 // NY), KV2 // NY), KV2 // NY)]
            block = lax.dot_general(columns, xin[...], (((0,), (0,)), ((), ())), preferred_element_type=jnp.float32)
            grad[i] = block.reshape(NX, NC, ROWS, COLS)
        core_copy[g] = remote(
            grad.at[pl.ds(2 * g, 2), :, 1 - c], core_in.at[g], core_send.at[0], core_recv.at[g], at(z, y, x, 1 - c)
        )

    slots = ((0, 3, 1, 2), (0, 1, 3, 2))
    first_to = (x_rel[1], x_rel[3])
    second_to = (x_rel[3], x_rel[1])

    def att_first(g):
        arrived(core_in.at[g], core_recv.at[g])
        for h in range(2):
            rows, cols = pl.ds(h * HALF, HALF), pl.ds(0, MAIN)
            for j in (2, 3):
                at_x = x_rel[slots[h][j]]
                for i in range(2):
                    send_a[g, h, j - 2, i] = grad[2 * g + i, at_x, c, rows, cols] + core_in[g, i, at_x, rows, cols]
            remote(send_a.at[g, h], recv_a.at[g, h], a_send.at[0], a_recv.at[g], at(z, y, first_to[h], c))
        for i in (2 * g, 2 * g + 1):
            d, cols = Y_ORDER[i], pl.ds(MAIN, COLS - MAIN)
            for at_x in range(NX):
                side[d, at_x] = grad[i, at_x, c, :, cols] + core_in[g, i - 2 * g, at_x, :, cols]
            if d:
                remote(side.at[d], side_in.at[d - 1], side_send.at[0], side_recv.at[0], at(z, lax.rem(y + d, NY), x, c))
        for h in range(2):
            rows, cols = pl.ds(h * HALF, HALF), pl.ds(0, MAIN)
            for j in (0, 1):
                at_x = x_rel[slots[h][j]]
                for i in range(2):
                    keep[g, h, j, i] = grad[2 * g + i, at_x, c, rows, cols] + core_in[g, i, at_x, rows, cols]

    def att_second(g):
        arrived(recv_a.at[g], a_recv.at[g])
        for h in range(2):
            send_b[g, h] = keep[g, h, 1] + recv_a[g, h, 1]
            remote(send_b.at[g, h], recv_b.at[g, h], b_send.at[0], b_recv.at[g], at(z, y, second_to[h], c))
        for h in range(2):
            keep_b[g, h] = keep[g, h, 0] + recv_a[g, h, 0]

    def att_third(g):
        arrived(recv_b.at[g], b_recv.at[g])
        for h in range(2):
            for i in range(2):
                y_out[2 * g + i, pl.ds(h * HALF, HALF)] = keep_b[g, h, i] + recv_b[g, h, i]
        for i in (2 * g, 2 * g + 1):
            d = Y_ORDER[i]
            if d:
                remote(y_out.at[i], y_in.at[d - 1], y_send.at[0], y_recv.at[0], at(z, lax.rem(y + d, NY), x, c))

    def att_cross(g):
        arrived(side_in, side_recv.at[0])
        total = side[0]
        for d in range(1, NY):
            total = total + side_in[d - 1]
        cross[...] = total
        for r in (2, 1, 3):
            remote(cross.at[x_rel[r]], cross_in.at[r - 1], cross_send.at[0], cross_recv.at[0], at(z, y, x_rel[r], c))

    def att_last(g):
        arrived(cross_in, cross_recv.at[0])
        total = cross[x]
        for r in range(1, NX):
            total = total + cross_in[r - 1]
        att_ref[:, pl.ds(MAIN, COLS - MAIN)] = total
        squares.append(squares_of(total))
        arrived(y_in, y_recv.at[0])
        total = y_out[Y_ORDER.index(0)]
        for d in range(1, NY):
            total = total + y_in[d - 1]
        att_ref[:, pl.ds(0, MAIN)] = total
        squares.append(squares_of(total))
        pltpu.make_async_copy(att_ref, att_hbm, out_sem.at[1]).start()

    work = {"second": att_second, "third": att_third, "cross": att_cross, "last": att_last}

    exp_piece(0)
    pl.semaphore_wait(barrier, len(greeted))
    ring_start(0, 0)
    exp_piece(2)
    ring_start(1, 2)
    exp_piece(1)
    ring_start(0, 1)
    exp_piece(3)
    ring_start(1, 3)
    ring_start(0, 2)
    ring_start(1, 0)
    ring_start(0, 3)
    ring_start(1, 1)
    att_group(0)
    att_group(1)
    att_group(2)
    att_group(3)
    for g in range(GROUPS):
        att_first(g)
    for n in range(len(STEPS)):
        ring_step(n)
        for name, g in BETWEEN.get(n, ()):
            work[name](g)

    value = squares[0]
    for other in squares[1:]:
        value = value + other
    norm_c[...] = jnp.sum(value, axis=0, keepdims=True)

    def norm_copy(n, src, dst, device):
        return pltpu.make_async_remote_copy(
            src_ref=src, dst_ref=dst, send_sem=norm_send.at[n], recv_sem=norm_recv.at[n],
            device_id=device, device_id_type=MESH,
        )

    for d in (4, 3, 5, 2, 6, 1, 7):
        norm_copy(0, norm_c, norm_z.at[d * NC + c], at(lax.rem(z + d, NZ), y, x, 1)).start()

    @pl.when(c == 0)
    def _():
        norm_copy(0, norm_c, norm_z.at[0], at(z, y, x, 1)).start()

    for ref, sem in (
        (ring, ring_send), (core_in, core_send), (send_a, a_send), (send_b, b_send), (y_in, y_send), (exp_ref, out_sem),
        (side_in, side_send), (cross_in, cross_send),
    ):
        arrived(ref, sem.at[0])
    arrived(att_ref, out_sem.at[1])

    @pl.when(c == 0)
    def _():
        sent = norm_z.at[pl.ds(0, NZ)]
        pltpu.make_async_copy(sent, sent, norm_send.at[0]).wait()
        pltpu.make_async_copy(norm_p, norm_p, norm_recv.at[1]).wait()

    @pl.when(c == 1)
    def _():
        norm_z[1] = norm_c[...]
        others = norm_z.at[pl.ds(0, NZ * NC - 1)]
        pltpu.make_async_copy(others, others, norm_recv.at[0]).wait()
        norm_p[0] = jnp.sum(norm_z[...], axis=0)
        plane = [(dy, dx) for dy in range(NY) for dx in range(NX) if dy or dx]
        plane.sort(key=lambda e: -min(e[0], NY - e[0]) - min(e[1], NX - e[1]))
        for dy, dx in plane:
            for core in range(NC):
                device = at(z, lax.rem(y + dy, NY), lax.rem(x + dx, NX), core)
                norm_copy(1, norm_p.at[0], norm_p.at[dy * NX + dx], device).start()
        norm_copy(1, norm_p.at[0], norm_p.at[0], at(z, y, x, 0)).start()
        sent = norm_z.at[pl.ds(0, NZ - 1)]
        pltpu.make_async_copy(sent, sent, norm_send.at[0]).wait()
        others = norm_p.at[pl.ds(1, NX * NY - 1)]
        pltpu.make_async_copy(others, others, norm_recv.at[1]).wait()
        for sent in (norm_p, others):
            pltpu.make_async_copy(sent, sent, norm_send.at[1]).wait()

    norm_ref[...] = jnp.sum(norm_p[...], axis=0)


def grads(hidden, cot, kv, xin, counts):
    f32, bf16 = jnp.float32, jnp.bfloat16
    dma = pltpu.SemaphoreType.DMA
    hbm = pl.BlockSpec(memory_space=pltpu.HBM)
    vmem = pl.BlockSpec(memory_space=pltpu.VMEM)
    return pl.pallas_call(
        grads_kernel,
        out_shape=tuple(jax.ShapeDtypeStruct(shape, f32) for shape in ((OWN, DW), (ROWS, COLS), (1, 128))),
        in_specs=[hbm] * 5,
        out_specs=(hbm, hbm, vmem),
        scratch_shapes=[
            pltpu.VMEM((OWN, DW), f32),
            pltpu.VMEM((ROWS, COLS), f32),
            pltpu.SMEM((1, 1), jnp.int32),
            pltpu.VMEM((HID, TOK), bf16),
            pltpu.VMEM((PIECES, TOK, WIDE), bf16),
            pltpu.VMEM((TOK, KV2), bf16),
            pltpu.VMEM((TOK, COLS), bf16),
            pltpu.VMEM((HID, TOK), bf16),
            pltpu.VMEM((PIECES, NZ, OWN, WIDE), f32),
            pltpu.VMEM((len(STEPS), 2, OWN, WIDE), f32),
            pltpu.VMEM((NY, NX, NC, ROWS, COLS), f32),
            pltpu.VMEM((GROUPS, 2, NX, ROWS, COLS), f32),
            pltpu.VMEM((GROUPS, 2, 2, 2, HALF, MAIN), f32),
            pltpu.VMEM((GROUPS, 2, 2, 2, HALF, MAIN), f32),
            pltpu.VMEM((GROUPS, 2, 2, 2, HALF, MAIN), f32),
            pltpu.VMEM((GROUPS, 2, 2, HALF, MAIN), f32),
            pltpu.VMEM((GROUPS, 2, 2, HALF, MAIN), f32),
            pltpu.VMEM((GROUPS, 2, 2, HALF, MAIN), f32),
            pltpu.VMEM((NY, ROWS, MAIN), f32),
            pltpu.VMEM((NY - 1, ROWS, MAIN), f32),
            pltpu.VMEM((NY, NX, ROWS, COLS - MAIN), f32),
            pltpu.VMEM((NY - 1, NX, ROWS, COLS - MAIN), f32),
            pltpu.VMEM((NX, ROWS, COLS - MAIN), f32),
            pltpu.VMEM((NX - 1, ROWS, COLS - MAIN), f32),
            pltpu.VMEM((1, 128), f32),
            pltpu.VMEM((NZ * NC, 1, 128), f32),
            pltpu.VMEM((NX * NY, 1, 128), f32),
            dma((4 + PIECES,)),
            dma((1,)),
            dma((len(STEPS),)),
            dma((1,)),
            dma((GROUPS,)),
            dma((1,)),
            dma((GROUPS,)),
            dma((1,)),
            dma((GROUPS,)),
            dma((1,)),
            dma((1,)),
            dma((1,)),
            dma((1,)),
            dma((1,)),
            dma((1,)),
            dma((2,)),
            dma((2,)),
            dma((2,)),
        ],
        compiler_params=pltpu.CompilerParams(
            collective_id=0, has_side_effects=True, vmem_limit_bytes=55091 * 1024
        ),
        name="grads",
    )(hidden, cot, kv, xin, counts)


BLOCKS = 4


def update_kernel(norm_hbm, *refs):
    att_in, exp_in, att_out, exp_out = refs[0:4], refs[4:8], refs[8:11], refs[11:14]
    norm, att, exp, new_att, new_exp, load_sem, store_sem = refs[14:]
    wide = DW // BLOCKS
    cols = [pl.ds(n * wide, wide) for n in range(BLOCKS)]
    pltpu.make_async_copy(norm_hbm, norm, load_sem.at[0]).start()
    for i, a in enumerate(att_in):
        pltpu.make_async_copy(a, att.at[i], load_sem.at[1]).start()
    for n in range(BLOCKS):
        for i, a in enumerate(exp_in):
            pltpu.make_async_copy(a.at[:, cols[n]], exp.at[i, :, cols[n]], load_sem.at[2 + n]).start()

    def arrived(ref, sem):
        pltpu.make_async_copy(ref, ref, sem).wait()

    def block(values, keep, sources, targets, sem):
        new = adam_update(*values, clip)
        for i in range(3):
            keep(i, new[i])
            pltpu.make_async_copy(sources[i], targets[i], sem).start()

    arrived(norm, load_sem.at[0])
    arrived(att, load_sem.at[1])
    entries = float(KV2 * D + NY * NX * NC // GROUP * FF * DW)
    square_sum = jnp.sum(norm[...], axis=1, keepdims=True)
    clip = jnp.minimum(1.0, jnp.sqrt(jnp.full_like(square_sum, entries)) / (jnp.sqrt(square_sum) + 1e-06))

    def keep_att(i, value):
        new_att[i] = value

    block([att[i] for i in range(4)], keep_att, [new_att.at[i] for i in range(3)], att_out, store_sem.at[0])
    for n in range(BLOCKS):
        arrived(exp.at[:, :, cols[n]], load_sem.at[2 + n])

        def keep_exp(i, value):
            new_exp[i, :, cols[n]] = value

        block(
            [exp[i, :, cols[n]] for i in range(4)],
            keep_exp,
            [new_exp.at[i, :, cols[n]] for i in range(3)],
            [ref.at[:, cols[n]] for ref in exp_out],
            store_sem.at[1],
        )
    arrived(new_att, store_sem.at[0])
    arrived(new_exp, store_sem.at[1])


def update(norm, att, exp):
    f32 = jnp.float32
    hbm = pl.BlockSpec(memory_space=pltpu.HBM)
    return pl.pallas_call(
        update_kernel,
        out_shape=tuple(jax.ShapeDtypeStruct(a.shape, f32) for a in (*att[:3], *exp[:3])),
        in_specs=[hbm] * 9,
        out_specs=(hbm,) * 6,
        scratch_shapes=[
            pltpu.VMEM((1, 128), f32),
            pltpu.VMEM((4, ROWS, COLS), f32),
            pltpu.VMEM((4, OWN, DW), f32),
            pltpu.VMEM((3, ROWS, COLS), f32),
            pltpu.VMEM((3, OWN, DW), f32),
            pltpu.SemaphoreType.DMA((2 + BLOCKS,)),
            pltpu.SemaphoreType.DMA((2,)),
        ],
        compiler_params=pltpu.CompilerParams(vmem_limit_bytes=55091 * 1024),
        name="update",
    )(norm, *att, *exp)


def on_device(
    att_input,
    kv_cotangent,
    expert_hidden,
    expert_cotangent,
    token_counts,
    att_param,
    att_moment,
    att_second,
    exp_param,
    exp_moment,
    exp_second,
):
    exp_grad, att_grad, norm = grads(expert_hidden.T, expert_cotangent, kv_cotangent, att_input, token_counts)
    return update(
        norm,
        (att_param, att_moment, att_second, att_grad),
        (exp_param, exp_moment, exp_second, exp_grad),
    )


def solution(mesh):
    in_specs = (
        P("dp", "expert"),
        P("dp", None),
        P("expert", "dp"),
        P("expert", "dp"),
        P("dp", "expert"),
        P("dp", "expert"),
        P("dp", "expert"),
        P("dp", "expert"),
        P(("dp", "expert"), None),
        P(("dp", "expert"), None),
        P(("dp", "expert"), None),
    )
    out_specs = (
        P("dp", "expert"),
        P("dp", "expert"),
        P("dp", "expert"),
        P(("dp", "expert"), None),
        P(("dp", "expert"), None),
        P(("dp", "expert"), None),
    )
    return jax.shard_map(
        on_device, mesh=mesh, in_specs=in_specs, out_specs=out_specs, check_vma=False
    )
```

```python
import functools

import jax
import jax.numpy as jnp
from jax import lax
from jax.experimental import pallas as pl
from jax.experimental.pallas import tpu as pltpu
from jax.sharding import PartitionSpec as P

D = 4096
KV2 = 1024
FF = 1536
DW = 2048
GROUP = 8

beta_one = 0.9
beta_two = 0.95
learn_rate = 0.01
decay_rate = 0.1
epsilon = 1e-08
step_number = 5

NX, NY, NZ, NC = 4, 8, 8, 2
TOK = 384
HID = 192
OWN = HID // NZ
HALVES = 2
SPLIT = 2
PIECES = HALVES * SPLIT
WIDE = DW // PIECES
DEPTH = NZ // 2
STEPS = [
    (DEPTH - (unit + 1) // 2, unit % 2 * SPLIT + p, (1 - unit % 2) * SPLIT + p)
    for unit in range(2 * DEPTH - 1)
    for p in range(SPLIT)
]
SLOTS = {(way, step[1 + way], step[0]): (n, way) for n, step in enumerate(STEPS) for way in range(2)}
COLS = 512
MAIN = COLS - 128
ROWS = 16
HALF = ROWS // 2
GROUPS = 4
Y_ORDER = (4, 3, 5, 2, 6, 1, 7, 0)
MESH = pl.DeviceIdType.MESH
RING, ATT, NORM = True, True, True
BETWEEN = {
    1: (('second', 0),),
    2: (('second', 1),),
    3: (('second', 2),),
    5: (('second', 3), ('third', 0)),
    6: (('third', 1),),
    7: (('third', 2), ('cross', 0)),
    8: (('third', 3),),
    11: (('last', 0),),
}


def adam_update(param, moment, second, grad, clip):
    scaled = clip * grad
    new_moment = beta_one * moment + (1.0 - beta_one) * scaled
    new_second = beta_two * second + (1.0 - beta_two) * scaled * scaled
    fix_one = 1.0 - beta_one**step_number
    fix_two = 1.0 - beta_two**step_number
    update = new_moment / fix_one / (jnp.sqrt(new_second / fix_two) + epsilon)
    new_param = param - learn_rate * (update + decay_rate * param)
    return (new_param, new_moment, new_second)


def grads_kernel(
    hidden_hbm, cot_hbm, kv_hbm, x_hbm, count_hbm,
    exp_hbm, att_hbm, norm_ref,
    exp_ref, att_ref, count_ref, hidden, cot, kv, xin, masked, part, ring, grad, core_in, keep, send_a, recv_a, keep_b, send_b, recv_b, y_out, y_in,
    side, side_in, cross, cross_in,
    norm_c, norm_z, norm_p,
    load_sem, ring_send, ring_recv, core_send, core_recv, a_send, a_recv, b_send, b_recv, y_send, y_recv, side_send, side_recv, cross_send, cross_recv, norm_send, norm_recv, out_sem,
):
    dp = lax.axis_index("dp")
    z = lax.axis_index("expert")
    c = lax.rem(dp, NC)
    x = lax.rem(dp // NC, NX)
    y = dp // (NC * NX)

    def at(zz, yy, xx, cc):
        return ((yy * NX + xx) * NC + cc, zz)

    x_rel = (x, x + 1 - 2 * lax.rem(x, 2), lax.rem(x + 2, NX), NX - 1 - x)

    barrier = pltpu.get_barrier_semaphore()
    greeted = [at(lax.rem(z + 1, NZ), y, x, c), at(lax.rem(z + NZ - 1, NZ), y, x, c), at(z, y, x, 1 - c)]
    greeted += [at(z, y, x_rel[r], c) for r in range(1, NX)]
    greeted += [at(z, lax.rem(y + d, NY), x, c) for d in range(1, NY)]
    for device in greeted:
        pl.semaphore_signal(barrier, inc=1, device_id=device, device_id_type=MESH)

    loads = [pltpu.make_async_copy(hidden_hbm, hidden, load_sem.at[0])]
    for k in range(PIECES):
        loads.append(pltpu.make_async_copy(cot_hbm.at[:, pl.ds(k * WIDE, WIDE)], cot.at[k], load_sem.at[1 + k]))
    loads.append(pltpu.make_async_copy(x_hbm, xin, load_sem.at[1 + PIECES]))
    loads.append(pltpu.make_async_copy(kv_hbm, kv, load_sem.at[2 + PIECES]))
    count_load = pltpu.make_async_copy(count_hbm, count_ref, load_sem.at[3 + PIECES])
    count_load.start()
    for n in (0, 1, 1 + SPLIT, 2, 2 + SPLIT, 1 + PIECES, 2 + PIECES):
        loads[n].start()

    def squares_of(value):
        rows, width = value.shape
        value = value * value
        total = value[0:8, 0:128]
        for i in range(0, rows, 8):
            for j in range(0, width, 128):
                if i or j:
                    total = total + value[i : i + 8, j : j + 128]
        return total

    def arrived(ref, sem):
        pltpu.make_async_copy(ref, ref, sem).wait()

    def remote(src, dst, send_sem, recv_sem, device):
        copy = pltpu.make_async_remote_copy(
            src_ref=src, dst_ref=dst, send_sem=send_sem, recv_sem=recv_sem, device_id=device, device_id_type=MESH
        )
        copy.start()
        return copy

    towards = (at(lax.rem(z + NZ - 1, NZ), y, x, c), at(lax.rem(z + 1, NZ), y, x, c))

    def shard(way, hops):
        return lax.rem(z + NZ - hops, NZ) if way == 0 else lax.rem(z + hops, NZ)

    def ring_send_step(way, k, hops, src):
        if not RING:
            return
        n, _ = SLOTS[way, k, hops]
        remote(src, ring.at[n, way], ring_send.at[0], ring_recv.at[n], towards[way])

    def ring_start(way, k):
        if not RING:
            return
        hops = DEPTH if k // SPLIT == way else DEPTH - 1
        ring_send_step(way, k, hops, part.at[k, shard(way, hops)])

    squares = []

    def ring_step(n):
        hops, down, up = STEPS[n]
        left = hops - 1
        arrived(ring.at[n], ring_recv.at[n])
        for way, k in enumerate((down, up)):
            if left:
                ring[n, way] = ring[n, way] + part[k, shard(way, left)]
                ring_send_step(way, k, left, ring.at[n, way])
                continue
            cols = pl.ds(k * WIDE, WIDE)
            if k // SPLIT != way:
                exp_ref[:, cols] = part[k, z] + ring[n, way]
            else:
                total = exp_ref[:, cols] + ring[n, way]
                exp_ref[:, cols] = total
                pltpu.make_async_copy(exp_ref.at[:, cols], exp_hbm.at[:, cols], out_sem.at[0]).start()
                squares.append(squares_of(total))

    count_load.wait()
    loads[0].wait()
    live = lax.broadcasted_iota(jnp.int32, (HID, TOK), 1) < count_ref[0, 0]
    masked[...] = jnp.where(live, hidden[...].astype(jnp.float32), 0.0).astype(jnp.bfloat16)

    def exp_piece(k):
        loads[1 + k].wait()
        block = lax.dot_general(
            masked[...], cot[k], (((1,), (0,)), ((), ())), preferred_element_type=jnp.float32
        )
        part[k] = block.reshape(NZ, OWN, WIDE)

    core_copy = {}

    def att_group(g):
        if not ATT:
            return
        if g == 0:
            loads[1 + PIECES].wait()
            loads[2 + PIECES].wait()
        for i in (2 * g, 2 * g + 1):
            target = lax.rem(y + Y_ORDER[i], NY)
            columns = kv[:, pl.ds(pl.multiple_of(target * (KV2 // NY), KV2 // NY), KV2 // NY)]
            block = lax.dot_general(columns, xin[...], (((0,), (0,)), ((), ())), preferred_element_type=jnp.float32)
            grad[i] = block.reshape(NX, NC, ROWS, COLS)
        core_copy[g] = remote(
            grad.at[pl.ds(2 * g, 2), :, 1 - c], core_in.at[g], core_send.at[0], core_recv.at[g], at(z, y, x, 1 - c)
        )

    slots = ((0, 3, 1, 2), (0, 1, 3, 2))
    first_to = (x_rel[1], x_rel[3])
    second_to = (x_rel[3], x_rel[1])

    def att_first(g):
        arrived(core_in.at[g], core_recv.at[g])
        for h in range(2):
            rows, cols = pl.ds(h * HALF, HALF), pl.ds(0, MAIN)
            for j in (2, 3):
                at_x = x_rel[slots[h][j]]
                for i in range(2):
                    send_a[g, h, j - 2, i] = grad[2 * g + i, at_x, c, rows, cols] + core_in[g, i, at_x, rows, cols]
            remote(send_a.at[g, h], recv_a.at[g, h], a_send.at[0], a_recv.at[g], at(z, y, first_to[h], c))
        for i in (2 * g, 2 * g + 1):
            d, cols = Y_ORDER[i], pl.ds(MAIN, COLS - MAIN)
            for at_x in range(NX):
                side[d, at_x] = grad[i, at_x, c, :, cols] + core_in[g, i - 2 * g, at_x, :, cols]
            if d:
                remote(side.at[d], side_in.at[d - 1], side_send.at[0], side_recv.at[0], at(z, lax.rem(y + d, NY), x, c))
        for h in range(2):
            rows, cols = pl.ds(h * HALF, HALF), pl.ds(0, MAIN)
            for j in (0, 1):
                at_x = x_rel[slots[h][j]]
                for i in range(2):
                    keep[g, h, j, i] = grad[2 * g + i, at_x, c, rows, cols] + core_in[g, i, at_x, rows, cols]

    def att_second(g):
        arrived(recv_a.at[g], a_recv.at[g])
        for h in range(2):
            send_b[g, h] = keep[g, h, 1] + recv_a[g, h, 1]
            remote(send_b.at[g, h], recv_b.at[g, h], b_send.at[0], b_recv.at[g], at(z, y, second_to[h], c))
        for h in range(2):
            keep_b[g, h] = keep[g, h, 0] + recv_a[g, h, 0]

    def att_third(g):
        arrived(recv_b.at[g], b_recv.at[g])
        for h in range(2):
            for i in range(2):
                y_out[2 * g + i, pl.ds(h * HALF, HALF)] = keep_b[g, h, i] + recv_b[g, h, i]
        for i in (2 * g, 2 * g + 1):
            d = Y_ORDER[i]
            if d:
                remote(y_out.at[i], y_in.at[d - 1], y_send.at[0], y_recv.at[0], at(z, lax.rem(y + d, NY), x, c))

    def att_cross(g):
        arrived(side_in, side_recv.at[0])
        total = side[0]
        for d in range(1, NY):
            total = total + side_in[d - 1]
        cross[...] = total
        for r in (2, 1, 3):
            remote(cross.at[x_rel[r]], cross_in.at[r - 1], cross_send.at[0], cross_recv.at[0], at(z, y, x_rel[r], c))

    def att_last(g):
        arrived(cross_in, cross_recv.at[0])
        total = cross[x]
        for r in range(1, NX):
            total = total + cross_in[r - 1]
        att_ref[:, pl.ds(MAIN, COLS - MAIN)] = total
        squares.append(squares_of(total))
        arrived(y_in, y_recv.at[0])
        total = y_out[Y_ORDER.index(0)]
        for d in range(1, NY):
            total = total + y_in[d - 1]
        att_ref[:, pl.ds(0, MAIN)] = total
        squares.append(squares_of(total))
        pltpu.make_async_copy(att_ref, att_hbm, out_sem.at[1]).start()

    work = {"second": att_second, "third": att_third, "cross": att_cross, "last": att_last}

    exp_piece(0)
    pl.semaphore_wait(barrier, len(greeted))
    ring_start(0, 0)
    exp_piece(2)
    ring_start(1, 2)
    exp_piece(1)
    ring_start(0, 1)
    exp_piece(3)
    ring_start(1, 3)
    ring_start(0, 2)
    ring_start(1, 0)
    ring_start(0, 3)
    ring_start(1, 1)
    att_group(0)
    att_group(1)
    att_group(2)
    att_group(3)
    for g in range(GROUPS):
        att_first(g)
    for n in range(len(STEPS)):
        ring_step(n)
        for name, g in BETWEEN.get(n, ()):
            work[name](g)

    value = squares[0]
    for other in squares[1:]:
        value = value + other
    norm_c[...] = jnp.sum(value, axis=0, keepdims=True)

    def norm_copy(n, src, dst, device):
        return pltpu.make_async_remote_copy(
            src_ref=src, dst_ref=dst, send_sem=norm_send.at[n], recv_sem=norm_recv.at[n],
            device_id=device, device_id_type=MESH,
        )

    plane = [(dy, dx) for dy in range(NY) for dx in range(NX) if dy or dx]
    plane.sort(key=lambda e: -min(e[0], NY - e[0]) - min(e[1], NX - e[1]))
    for dy, dx in plane:
        device = at(z, lax.rem(y + dy, NY), lax.rem(x + dx, NX), 1)
        norm_copy(0, norm_c, norm_p.at[(dy * NX + dx) * NC + c], device).start()

    @pl.when(c == 0)
    def _():
        norm_copy(0, norm_c, norm_p.at[0], at(z, y, x, 1)).start()

    for ref, sem in (
        (ring, ring_send), (core_in, core_send), (send_a, a_send), (send_b, b_send), (y_in, y_send), (exp_ref, out_sem),
        (side_in, side_send), (cross_in, cross_send),
    ):
        arrived(ref, sem.at[0])
    arrived(att_ref, out_sem.at[1])

    @pl.when(c == 0)
    def _():
        arrived(norm_p.at[pl.ds(0, NX * NY)], norm_send.at[0])
        arrived(norm_z, norm_recv.at[1])

    @pl.when(c == 1)
    def _():
        norm_p[1] = norm_c[...]
        arrived(norm_p.at[pl.ds(0, NX * NY * NC - 1)], norm_recv.at[0])
        norm_z[0] = jnp.sum(norm_p[...], axis=0)
        for d in (4, 3, 5, 2, 6, 1, 7):
            for core in range(NC):
                norm_copy(1, norm_z.at[0], norm_z.at[d], at(lax.rem(z + d, NZ), y, x, core)).start()
        norm_copy(1, norm_z.at[0], norm_z.at[0], at(z, y, x, 0)).start()
        arrived(norm_p.at[pl.ds(0, NX * NY - 1)], norm_send.at[0])
        others = norm_z.at[pl.ds(1, NZ - 1)]
        arrived(others, norm_recv.at[1])
        arrived(norm_z, norm_send.at[1])
        arrived(others, norm_send.at[1])

    norm_ref[...] = jnp.sum(norm_z[...], axis=0)


def grads(hidden, cot, kv, xin, counts):
    f32, bf16 = jnp.float32, jnp.bfloat16
    dma = pltpu.SemaphoreType.DMA
    hbm = pl.BlockSpec(memory_space=pltpu.HBM)
    vmem = pl.BlockSpec(memory_space=pltpu.VMEM)
    return pl.pallas_call(
        grads_kernel,
        out_shape=tuple(jax.ShapeDtypeStruct(shape, f32) for shape in ((OWN, DW), (ROWS, COLS), (1, 128))),
        in_specs=[hbm] * 5,
        out_specs=(hbm, hbm, vmem),
        scratch_shapes=[
            pltpu.VMEM((OWN, DW), f32),
            pltpu.VMEM((ROWS, COLS), f32),
            pltpu.SMEM((1, 1), jnp.int32),
            pltpu.VMEM((HID, TOK), bf16),
            pltpu.VMEM((PIECES, TOK, WIDE), bf16),
            pltpu.VMEM((TOK, KV2), bf16),
            pltpu.VMEM((TOK, COLS), bf16),
            pltpu.VMEM((HID, TOK), bf16),
            pltpu.VMEM((PIECES, NZ, OWN, WIDE), f32),
            pltpu.VMEM((len(STEPS), 2, OWN, WIDE), f32),
            pltpu.VMEM((NY, NX, NC, ROWS, COLS), f32),
            pltpu.VMEM((GROUPS, 2, NX, ROWS, COLS), f32),
            pltpu.VMEM((GROUPS, 2, 2, 2, HALF, MAIN), f32),
            pltpu.VMEM((GROUPS, 2, 2, 2, HALF, MAIN), f32),
            pltpu.VMEM((GROUPS, 2, 2, 2, HALF, MAIN), f32),
            pltpu.VMEM((GROUPS, 2, 2, HALF, MAIN), f32),
            pltpu.VMEM((GROUPS, 2, 2, HALF, MAIN), f32),
            pltpu.VMEM((GROUPS, 2, 2, HALF, MAIN), f32),
            pltpu.VMEM((NY, ROWS, MAIN), f32),
            pltpu.VMEM((NY - 1, ROWS, MAIN), f32),
            pltpu.VMEM((NY, NX, ROWS, COLS - MAIN), f32),
            pltpu.VMEM((NY - 1, NX, ROWS, COLS - MAIN), f32),
            pltpu.VMEM((NX, ROWS, COLS - MAIN), f32),
            pltpu.VMEM((NX - 1, ROWS, COLS - MAIN), f32),
            pltpu.VMEM((1, 128), f32),
            pltpu.VMEM((NZ, 1, 128), f32),
            pltpu.VMEM((NX * NY * NC, 1, 128), f32),
            dma((4 + PIECES,)),
            dma((1,)),
            dma((len(STEPS),)),
            dma((1,)),
            dma((GROUPS,)),
            dma((1,)),
            dma((GROUPS,)),
            dma((1,)),
            dma((GROUPS,)),
            dma((1,)),
            dma((1,)),
            dma((1,)),
            dma((1,)),
            dma((1,)),
            dma((1,)),
            dma((2,)),
            dma((2,)),
            dma((2,)),
        ],
        compiler_params=pltpu.CompilerParams(
            collective_id=0, has_side_effects=True, vmem_limit_bytes=55091 * 1024
        ),
        name="grads",
    )(hidden, cot, kv, xin, counts)


BLOCKS = 4


def update_kernel(norm_hbm, *refs):
    att_in, exp_in, att_out, exp_out = refs[0:4], refs[4:8], refs[8:11], refs[11:14]
    norm, att, exp, new_att, new_exp, load_sem, store_sem = refs[14:]
    wide = DW // BLOCKS
    cols = [pl.ds(n * wide, wide) for n in range(BLOCKS)]
    for n in range(BLOCKS):
        for i, a in enumerate(exp_in):
            pltpu.make_async_copy(a.at[:, cols[n]], exp.at[i, :, cols[n]], load_sem.at[2 + n]).start()
    pltpu.make_async_copy(norm_hbm, norm, load_sem.at[0]).start()
    for i, a in enumerate(att_in):
        pltpu.make_async_copy(a, att.at[i], load_sem.at[1]).start()

    def arrived(ref, sem):
        pltpu.make_async_copy(ref, ref, sem).wait()

    def block(values, keep, sources, targets, sem):
        new = adam_update(*values, clip)
        for i in range(3):
            keep(i, new[i])
            pltpu.make_async_copy(sources[i], targets[i], sem).start()

    arrived(norm, load_sem.at[0])
    arrived(att, load_sem.at[1])
    entries = float(KV2 * D + NY * NX * NC // GROUP * FF * DW)
    square_sum = jnp.sum(norm[...], axis=1, keepdims=True)
    clip = jnp.minimum(1.0, jnp.sqrt(jnp.full_like(square_sum, entries)) / (jnp.sqrt(square_sum) + 1e-06))

    def keep_att(i, value):
        new_att[i] = value

    block([att[i] for i in range(4)], keep_att, [new_att.at[i] for i in range(3)], att_out, store_sem.at[0])
    for n in range(BLOCKS):
        arrived(exp.at[:, :, cols[n]], load_sem.at[2 + n])

        def keep_exp(i, value):
            new_exp[i, :, cols[n]] = value

        block(
            [exp[i, :, cols[n]] for i in range(4)],
            keep_exp,
            [new_exp.at[i, :, cols[n]] for i in range(3)],
            [ref.at[:, cols[n]] for ref in exp_out],
            store_sem.at[1],
        )
    arrived(new_att, store_sem.at[0])
    arrived(new_exp, store_sem.at[1])


def update(norm, att, exp):
    f32 = jnp.float32
    hbm = pl.BlockSpec(memory_space=pltpu.HBM)
    return pl.pallas_call(
        update_kernel,
        out_shape=tuple(jax.ShapeDtypeStruct(a.shape, f32) for a in (*att[:3], *exp[:3])),
        in_specs=[hbm] * 9,
        out_specs=(hbm,) * 6,
        scratch_shapes=[
            pltpu.VMEM((1, 128), f32),
            pltpu.VMEM((4, ROWS, COLS), f32),
            pltpu.VMEM((4, OWN, DW), f32),
            pltpu.VMEM((3, ROWS, COLS), f32),
            pltpu.VMEM((3, OWN, DW), f32),
            pltpu.SemaphoreType.DMA((2 + BLOCKS,)),
            pltpu.SemaphoreType.DMA((2,)),
        ],
        compiler_params=pltpu.CompilerParams(vmem_limit_bytes=55091 * 1024),
        name="update",
    )(norm, *att, *exp)


def on_device(
    att_input,
    kv_cotangent,
    expert_hidden,
    expert_cotangent,
    token_counts,
    att_param,
    att_moment,
    att_second,
    exp_param,
    exp_moment,
    exp_second,
):
    exp_grad, att_grad, norm = grads(expert_hidden.T, expert_cotangent, kv_cotangent, att_input, token_counts)
    return update(
        norm,
        (att_param, att_moment, att_second, att_grad),
        (exp_param, exp_moment, exp_second, exp_grad),
    )


def solution(mesh):
    in_specs = (
        P("dp", "expert"),
        P("dp", None),
        P("expert", "dp"),
        P("expert", "dp"),
        P("dp", "expert"),
        P("dp", "expert"),
        P("dp", "expert"),
        P("dp", "expert"),
        P(("dp", "expert"), None),
        P(("dp", "expert"), None),
        P(("dp", "expert"), None),
    )
    out_specs = (
        P("dp", "expert"),
        P("dp", "expert"),
        P("dp", "expert"),
        P(("dp", "expert"), None),
        P(("dp", "expert"), None),
        P(("dp", "expert"), None),
    )
    return jax.shard_map(
        on_device, mesh=mesh, in_specs=in_specs, out_specs=out_specs, check_vma=False
    )
```
